32 devices in a mesh: seq: 16 (over z, y, x), row: 2 (over core).
Axes of the slice: x: 2, y: 2, z: 4, core: 2. Of those that a mesh axis runs over, the one named last changes fastest.
Arguments:
- tokens: bfloat16 [4, 2048, 768], P('row', 'seq'), may hold values from -6 to 6
- cotangent: bfloat16 [4, 2048, 768], P('row', 'seq'), may hold values from -6 to 6
- doc_lengths: int32 [4, 8], P('row'), may hold values from 1 to 2041, as said below
- attn_gain: float32 [768], replicated, may hold values from 0.5 to 1.5
- ema_beta: float32 [16, 768], replicated, may hold values from -6 to 6
- alpha_raw: float32 [16, 768], replicated, may hold values from -12 to 1.5
- delta_raw: float32 [16, 768], replicated, may hold values from -12 to 0
- ema_eta: float32 [16, 768], replicated, may hold values from -1.5 to 1.5
- ema_omega: float32 [768], replicated, may hold values from -6 to 6
- w_value: bfloat16 [768, 1536], replicated, may hold values from -0.21875 to 0.21875
- w_mix: bfloat16 [768, 3200], replicated, may hold values from -0.21875 to 0.21875
- query_gain: float32 [128], replicated, may hold values from -16 to 16
- query_bias: float32 [128], replicated, may hold values from -6 to 6
- key_gain: float32 [128], replicated, may hold values from -16 to 16
- w_out: bfloat16 [1536, 768], replicated, may hold values from -0.625 to 0.625
- ffn_gain: float32 [768], replicated, may hold values from 0.5 to 1.5
- w_up: bfloat16 [768, 1536], replicated, may hold values from -0.21875 to 0.21875
- w_down: bfloat16 [1536, 768], replicated, may hold values from -0.15625 to 0.15625
Outputs:
- output: bfloat16 [4, 2048, 768], P('row', 'seq')
- grad_tokens: float32 [4, 2048, 768], P('row', 'seq')
- grad_attn_gain: float32 [768], replicated
- grad_ema_beta: float32 [16, 768], replicated
- grad_alpha_raw: float32 [16, 768], replicated
- grad_delta_raw: float32 [16, 768], replicated
- grad_ema_eta: float32 [16, 768], replicated
- grad_ema_omega: float32 [768], replicated
- grad_w_value: float32 [768, 1536], replicated
- grad_w_mix: float32 [768, 3200], replicated
- grad_query_gain: float32 [128], replicated
- grad_query_bias: float32 [128], replicated
- grad_key_gain: float32 [128], replicated
- grad_w_out: float32 [1536, 768], replicated
- grad_ffn_gain: float32 [768], replicated
- grad_w_up: float32 [768, 1536], replicated
- grad_w_down: float32 [1536, 768], replicated
The draws below stay inside these ranges and needn't reach their ends.
Inputs may be any that keep to these rules, and one draw needn't show every extreme that they name: `doc_lengths`: each row's 8 lengths sum to 2048; in every row one document, at a place drawn from the seed, starts within the first 128 positions and ends within the last 128. In the first row all other documents have length 1.
All inputs are finite; a program needn't handle non-finite values.
Results may differ from the reference program's by a relative error of at most 0.028.
The reference program's roundings to bfloat16 on the way count: a program that leaves them out, or rounds other values in their place, can miss the bound.
Values may be sent and summed in bfloat16 or wider, within the bound.
No kernel may reach another device: no remote copies, remote signals or barrier semaphores. Data moves between devices by JAX's collectives and lax.ppermute only.
A program may use at most 320 MiB of HBM per device.

```python
import math
import jax
import jax.numpy as jnp
from jax import lax

D = 768
Z = 128
V = 1536
FF = 1536
EXP = 16
SEG = 128
NDOC = 8
LEN = 2048
ROWS = 4


def ema_rates(key):
    base_key = jax.random.fold_in(key, 17)
    rate_key, spread_key = jax.random.split(base_key)
    lowest = 0.02 / LEN
    highest = 1.0 / 15.0
    decay_rate = jnp.exp(jax.random.uniform(rate_key, (EXP, D), jnp.float32, jnp.log(lowest), jnp.log(highest)))
    spread_factor = jnp.exp(jax.random.uniform(spread_key, (EXP, D), jnp.float32, jnp.log(0.5), jnp.log(2.0)))
    input_rate = jnp.sqrt(2.0 * decay_rate) * spread_factor
    return (input_rate, decay_rate / input_rate)


def draw_alpha_raw(key, part):
    result = ema_rates(key)
    return jnp.log(result[0]) - jnp.log1p(-result[0])


def draw_delta_raw(key, part):
    result = ema_rates(key)
    return jnp.log(result[1]) - jnp.log1p(-result[1])


def draw_doc_lengths(key, part):
    count_key, place_key = jax.random.split(jax.random.fold_in(key, 29))
    ceiling = max(1, (SEG - 1) // (NDOC - 1))
    shorts = jax.random.randint(count_key, (ROWS, NDOC), 1, ceiling + 1, dtype=jnp.int32)
    first_row = jnp.arange(ROWS, dtype=jnp.int32)[:, None] == 0
    shorts = jnp.where(first_row, 1, shorts).astype(jnp.int32)
    places = jax.random.randint(place_key, (ROWS, 1), 0, NDOC, dtype=jnp.int32)
    columns = jnp.arange(NDOC, dtype=jnp.int32)[None, :]
    chosen = columns == places
    others = jnp.sum(jnp.where(chosen, 0, shorts), axis=1, keepdims=True)
    return jnp.where(chosen, LEN - others, shorts).astype(jnp.int32)


def block_levels(own_key, shape, cuts, least, largest):
    level, own = 1.0, jax.random.fold_in(own_key, 6)
    for position, blocks in cuts:
        heights = jnp.exp(jax.random.uniform(jax.random.fold_in(own, position), (blocks,), jnp.float32, least / len(cuts), largest / len(cuts)))
        level = level * jnp.repeat(heights, shape[position] // blocks).reshape([-1 if axis == position else 1 for axis in range(len(shape))])
    return level


def gaussian(key, extent, spread, limit, cuts=(), held_as=jnp.bfloat16):
    values = spread * jax.random.normal(key, extent, jnp.float32)
    if cuts:
        values = values * block_levels(key, extent, cuts, -0.22, 0.18)
    return jnp.clip(values, -limit, limit).astype(held_as)


def setup_inputs(seed: int = 0) -> dict:
    seeds = jax.random.split(jax.random.key(seed), 19)
    tokens = gaussian(seeds[0], (ROWS, LEN, D), 1.0, 6.0, ((0, 2), (1, 16)))
    cotangent = gaussian(seeds[1], (ROWS, LEN, D), 1.0, 6.0, ((0, 2), (1, 16)))
    doc_lengths = draw_doc_lengths(jax.random.fold_in(seeds[18], 71), 0)
    attn_gain = jnp.clip(1.0 + 0.1 * jax.random.normal(seeds[3], (D,), jnp.float32), 0.5, 1.5)
    ema_beta = gaussian(seeds[4], (EXP, D), 1.0, 6.0, (), jnp.float32)
    alpha_raw = draw_alpha_raw(jax.random.fold_in(seeds[18], 71), 0)
    delta_raw = draw_delta_raw(jax.random.fold_in(seeds[18], 71), 0)
    ema_eta = gaussian(seeds[7], (EXP, D), EXP ** -0.5, 1.5, (), jnp.float32)
    ema_omega = gaussian(seeds[8], (D,), 1.0, 6.0, (), jnp.float32)
    w_value = gaussian(seeds[9], (D, V), D ** -0.5, 0.21875)
    w_mix = gaussian(seeds[10], (D, Z + V + 2 * D), D ** -0.5, 0.21875)
    query_gain = gaussian(seeds[11], (Z,), 3.0, 16.0, (), jnp.float32)
    query_bias = gaussian(seeds[12], (Z,), 1.0, 6.0, (), jnp.float32)
    key_gain = gaussian(seeds[13], (Z,), 3.0, 16.0, (), jnp.float32)
    w_out = gaussian(seeds[14], (V, D), (V // 16) ** -0.5, 0.625)
    ffn_gain = jnp.clip(1.0 + 0.1 * jax.random.normal(seeds[15], (D,), jnp.float32), 0.5, 1.5)
    w_up = gaussian(seeds[16], (D, FF), D ** -0.5, 0.21875)
    w_down = gaussian(seeds[17], (FF, D), FF ** -0.5, 0.15625)
    return dict(tokens=tokens, cotangent=cotangent, doc_lengths=doc_lengths, attn_gain=attn_gain, ema_beta=ema_beta, alpha_raw=alpha_raw, delta_raw=delta_raw, ema_eta=ema_eta, ema_omega=ema_omega, w_value=w_value, w_mix=w_mix, query_gain=query_gain, query_bias=query_bias, key_gain=key_gain, w_out=w_out, ffn_gain=ffn_gain, w_up=w_up, w_down=w_down)


EPSILON = 1e-05
MASKED_SCORE = -1e+30
PRECISE = lax.Precision.HIGHEST

@jax.custom_vjp
def low(v):
    return lax.optimization_barrier(v.astype(jnp.bfloat16)).astype(jnp.float32)

@jax.custom_vjp
def low_back(v):
    return v

def low_keep(v):
    return (low(v), None)

def low_pass(kept, grad):
    return (grad,)

def back_keep(v):
    return (v, None)

def back_low(kept, grad):
    return (low(grad),)
low.defvjp(low_keep, low_pass)
low_back.defvjp(back_keep, back_low)

def matmul(left, right):
    return jnp.dot(left, right, precision=PRECISE, preferred_element_type=jnp.float32)

def layer_norm(inputs, gain):
    centred = inputs - lax.optimization_barrier(jnp.mean(inputs, axis=-1, keepdims=True))
    variance = lax.optimization_barrier(jnp.mean(centred * centred, axis=-1, keepdims=True))
    return centred * lax.rsqrt(variance + EPSILON) * gain

def ema_forward(normed, keeping, ema_alpha, ema_delta, ema_beta, ema_eta, ema_omega):
    decay_rate = 1.0 - ema_alpha * ema_delta
    feed_gain = ema_alpha * ema_beta
    block_len = math.gcd(LEN, 128)

    def advance(carried, inputs):
        row_in, flag = inputs
        carried = flag * decay_rate * carried + feed_gain * row_in[None, :]
        return (carried, lax.optimization_barrier(jnp.sum(ema_eta * carried, axis=0)) + ema_omega * row_in)

    @jax.checkpoint
    def run_block(carried, inputs):
        return lax.scan(advance, carried, inputs)
    blocks_in = (normed.reshape(LEN // block_len, block_len, D), keeping.reshape(LEN // block_len, block_len))
    _, outputs = lax.scan(run_block, jnp.zeros((EXP, D), jnp.float32), blocks_in)
    return outputs.reshape(LEN, D)

def attention_row(queries, keys, values, docs):
    scale_factor = Z ** (-0.5)
    rows_block = math.gcd(LEN, 512)
    positions = jnp.arange(LEN, dtype=jnp.int32)

    @jax.checkpoint
    def one_block(inputs):
        query_rows, query_pos, query_doc = inputs
        raw_scores = low_back(matmul(query_rows, keys.T))
        visible = (docs[None, :] == query_doc[:, None]) & (positions[None, :] <= query_pos[:, None])
        masked = jnp.where(visible, raw_scores * scale_factor, MASKED_SCORE)
        highest = lax.optimization_barrier(jnp.max(masked, axis=1, keepdims=True))
        total = lax.optimization_barrier(jnp.sum(jnp.where(visible, jnp.exp(masked - highest), 0.0), axis=1, keepdims=True))
        log_total = highest + jnp.log(total)
        probs = jnp.where(visible, jnp.exp(masked - log_total), 0.0)
        return matmul(low(probs), values)
    blocks = LEN // rows_block
    result = lax.map(one_block, (queries.reshape(blocks, rows_block, Z), positions.reshape(blocks, rows_block), docs.reshape(blocks, rows_block)))
    return result.reshape(LEN, V)

def forward_row(row_x, docs, keeping, weights):
    attn_gain, ema_beta, alpha_raw, delta_raw, ema_eta, ema_omega, w_value, w_mix, query_gain, query_bias, key_gain, w_out, ffn_gain, w_up, w_down = weights
    normed = layer_norm(row_x, attn_gain)
    ema_alpha = jax.nn.sigmoid(alpha_raw)
    ema_delta = jax.nn.sigmoid(delta_raw)
    smoothed = ema_forward(normed, keeping, ema_alpha, ema_delta, ema_beta, ema_eta, ema_omega)
    mixed_in = low(jax.nn.silu(smoothed))
    mixed = matmul(mixed_in, w_mix)
    heads = low_back(mixed[:, :Z + V + D])
    shared = jax.nn.silu(heads[:, :Z])
    reset_gate = jax.nn.silu(heads[:, Z:Z + V])
    update_gate = jax.nn.sigmoid(heads[:, Z + V:])
    queries = low(shared * query_gain + query_bias)
    keys = low(shared * key_gain)
    values = low(jax.nn.silu(low_back(matmul(low(normed), w_value))))
    attended = low_back(attention_row(queries, keys, values, docs))
    gated = low(reset_gate * attended)
    summed = low_back(mixed[:, Z + V + D:] + matmul(gated, w_out))
    after_attn = row_x + update_gate * (jax.nn.silu(summed) - row_x)
    ffn_in = low(layer_norm(after_attn, ffn_gain))
    hidden = low(jax.nn.silu(low_back(matmul(ffn_in, w_up))))
    return after_attn + matmul(hidden, w_down)

def reference(tokens, cotangent, doc_lengths, attn_gain, ema_beta, alpha_raw, delta_raw, ema_eta, ema_omega, w_value, w_mix, query_gain, query_bias, key_gain, w_out, ffn_gain, w_up, w_down):
    params = tuple((weight.astype(jnp.float32) for weight in (attn_gain, ema_beta, alpha_raw, delta_raw, ema_eta, ema_omega, w_value, w_mix, query_gain, query_bias, key_gain, w_out, ffn_gain, w_up, w_down)))
    positions = jnp.arange(LEN, dtype=jnp.int32)

    def per_row(totals, inputs):
        row_x, row_cot, lengths = inputs
        starts = (jnp.cumsum(lengths, dtype=jnp.int32) - lengths).astype(jnp.int32)
        docs = lax.optimization_barrier(jnp.sum((starts[:, None] <= positions[None, :]).astype(jnp.int32), axis=0)) - 1
        keeping = 1.0 - lax.optimization_barrier(jnp.sum((starts[:, None] == positions[None, :]).astype(jnp.float32), axis=0))

        def closed(inputs_x, *weights):
            return forward_row(inputs_x, docs, keeping, weights)
        result, pullback = jax.vjp(closed, row_x, *params)
        grads = pullback(row_cot)
        totals = tuple((total + grad for total, grad in zip(totals, grads[1:])))
        return (totals, (result.astype(jnp.bfloat16), grads[0]))
    start_totals = tuple((jnp.zeros_like(weight) for weight in params))
    totals, (outputs, grad_tokens) = lax.scan(per_row, start_totals, (tokens.astype(jnp.float32), cotangent.astype(jnp.float32), doc_lengths))
    return (outputs, grad_tokens, totals[0], totals[1], totals[2], totals[3], totals[4], totals[5], totals[6], totals[7], totals[8], totals[9], totals[10], totals[11], totals[12], totals[13], totals[14])
```

```python
import functools

import jax
import jax.numpy as jnp
from jax import lax
from jax.experimental import pallas as pl
from jax.experimental.pallas import tpu as pltpu
from jax.sharding import Mesh
from jax.sharding import PartitionSpec as P

EPSILON = 1e-05
MASKED_SCORE = -1e30
BF16 = jnp.bfloat16
F32 = jnp.float32
EVERY = ("g", "s", "core")
MIB = 1024 * 1024
BRIEF = pl.CostEstimate(flops=1, bytes_accessed=1, transcendentals=0)


def logistic(inputs):
    return 0.5 * jnp.tanh(0.5 * inputs) + 0.5


def silu_slope(inputs):
    gate = logistic(inputs)
    return gate * (1.0 + inputs * (1.0 - gate))


def norm_parts(inputs):
    centred = inputs - jnp.mean(inputs, axis=-1, keepdims=True)
    inverse = lax.rsqrt(jnp.mean(centred * centred, axis=-1, keepdims=True) + EPSILON)
    return (centred * inverse, inverse)


def norm_back(upstream, normed, inverse, gain):
    scaled = upstream * gain
    first_mean = jnp.mean(scaled, axis=-1, keepdims=True)
    second_mean = jnp.mean(scaled * normed, axis=-1, keepdims=True)
    return (
        inverse * (scaled - first_mean - normed * second_mean),
        jnp.sum(upstream * normed, axis=0),
    )


def dot(left, right, contract):
    return lax.dot_general(left, right, (contract, ((), ())), preferred_element_type=F32)


SMEM = functools.partial(pl.BlockSpec, memory_space=pltpu.SMEM)


def whole(*shape):
    return pl.BlockSpec(shape, lambda *_: (0,) * len(shape))


def first_kernel(keep_ref, x_ref, gain_ref, decay_ref, feed_ref, normed_ref, last_ref):
    segs, length, width = x_ref.shape
    for i in range(segs):
        normed_ref[i] = norm_parts(x_ref[i].astype(F32))[0] * gain_ref[...]
    part = width // 2
    for c in range(0, width, part):
        cols = slice(c, c + part)
        decay, feed = decay_ref[:, cols], feed_ref[:, cols]

        def eight(block, states):
            at = pl.multiple_of(block * 8, 8)
            rows = [normed_ref[i, pl.ds(at, 8), cols] for i in range(segs)]
            for u in range(8):
                states = tuple(
                    state * (decay * keep_ref[i, at + u]) + feed * rows[i][u : u + 1]
                    for i, state in enumerate(states)
                )
            return states

        zero = jnp.zeros(decay.shape, F32)
        states = lax.fori_loop(0, length // 8, eight, (zero,) * segs)
        for i in range(segs):
            last_ref[i, :, cols] = states[i]


def ema_first(keep, x, gain, decay, feed):
    segs, length, width = x.shape
    return pl.pallas_call(
        first_kernel,
        out_shape=(
            jax.ShapeDtypeStruct(x.shape, F32),
            jax.ShapeDtypeStruct((segs, *decay.shape), F32),
        ),
        in_specs=[SMEM()] + [pl.BlockSpec(memory_space=pltpu.VMEM)] * 4,
        out_specs=(pl.BlockSpec(memory_space=pltpu.VMEM),) * 2,
        compiler_params=pltpu.CompilerParams(vmem_limit_bytes=8 * MIB),
        cost_estimate=BRIEF,
        name="ema_first",
    )(keep, x, gain, decay, feed)


def second_kernel(
    place_ref, slot_ref, pass_ref, keep_ref, normed_ref, ends_ref, long_ref, decay_ref, feed_ref, eta_ref, omega_ref,
    smoothed_ref, mixed_ref, enter_ref,
):
    segs, length, width = normed_ref.shape
    for i in range(segs):

        def hop(p, state):
            return state * (long_ref[...] * pass_ref[p]) + ends_ref[slot_ref[p]]

        enter_ref[i] = lax.fori_loop(0, place_ref[i], hop, jnp.zeros(decay_ref.shape, F32))

    part = width // 2
    for c in range(0, width, part):
        cols = slice(c, c + part)
        decay, feed, eta = decay_ref[:, cols], feed_ref[:, cols], eta_ref[:, cols]
        omega = omega_ref[:, cols]

        def eight(block, states):
            at = pl.multiple_of(block * 8, 8)
            rows = [normed_ref[i, pl.ds(at, 8), cols] for i in range(segs)]
            sums = [[] for _ in range(segs)]
            for u in range(8):
                following = []
                for i, state in enumerate(states):
                    state = state * (decay * keep_ref[i, at + u]) + feed * rows[i][u : u + 1]
                    sums[i].append(jnp.sum(eta * state, axis=0, keepdims=True))
                    following.append(state)
                states = tuple(following)
            for i in range(segs):
                smooth = jnp.concatenate(sums[i], axis=0) + omega * rows[i]
                smoothed_ref[i, pl.ds(at, 8), cols] = smooth
            return states

        lax.fori_loop(0, length // 8, eight, tuple(enter_ref[i, :, cols] for i in range(segs)))
    smoothed = smoothed_ref[...]
    mixed_ref[...] = (smoothed * logistic(smoothed)).astype(BF16)


VMEM = functools.partial(pl.BlockSpec, memory_space=pltpu.VMEM)


def ema_second(place, slots, passes, keep, normed, ends, long_decay, decay, feed, eta, omega):
    segs, length, width = normed.shape
    return pl.pallas_call(
        second_kernel,
        out_shape=(
            jax.ShapeDtypeStruct(normed.shape, F32),
            jax.ShapeDtypeStruct(normed.shape, BF16),
            jax.ShapeDtypeStruct((segs, *decay.shape), F32),
        ),
        in_specs=[SMEM()] * 4 + [VMEM()] * 7,
        out_specs=(VMEM(),) * 3,
        compiler_params=pltpu.CompilerParams(vmem_limit_bytes=12 * MIB),
        cost_estimate=BRIEF,
        name="ema_second",
    )(place, slots, passes, keep, normed, ends, long_decay, decay, feed, eta, omega)


def fourth_kernel(
    place_ref, slot_ref, pass_ref, keep_ref, next_ref, d_ref, normed_ref, enter_ref, heads_ref, long_ref,
    decay_ref, feed_ref, eta_ref, omega_ref, alpha_ref, delta_ref, beta_ref, omega_grad_ref, grad_ref, rates_ref, before_ref,
):
    segs, length, width = normed_ref.shape
    n_heads = decay_ref.shape[0]
    half = width // 2
    for c in range(0, width, half):
        cols = slice(c, c + half)
        decay, feed = decay_ref[:, cols], feed_ref[:, cols]

        def again(block, states):
            at = pl.multiple_of(block * 8, 8)
            rows = [normed_ref[i, pl.ds(at, 8), cols] for i in range(segs)]
            for u in range(8):
                following = []
                for i, state in enumerate(states):
                    state = state * keep_ref[i, at + u]
                    before_ref[i, at + u, :, cols] = state
                    following.append(state * decay + feed * rows[i][u : u + 1])
                states = tuple(following)
            return states

        lax.fori_loop(0, length // 8, again, tuple(enter_ref[i, :, cols] for i in range(segs)))

    count = slot_ref.shape[0]
    part = width // 3
    for c in range(0, width, part):
        cols = slice(c, c + part)
        decay, feed, eta = decay_ref[:, cols], feed_ref[:, cols], eta_ref[:, cols]
        omega = omega_ref[:, cols]
        entering = []
        for i in range(segs):

            def hop(back, grad):
                p = count - 1 - back
                return grad * (long_ref[:, cols] * pass_ref[p]) + heads_ref[slot_ref[p], :, cols]

            entering.append(lax.fori_loop(0, count - 1 - place_ref[i], hop, jnp.zeros(decay.shape, F32)))

        def eight(block, carried):
            grads, kept, decayed, fed = carried
            at = pl.multiple_of(length - 8 - block * 8, 8)
            rows = [normed_ref[i, pl.ds(at, 8), cols] for i in range(segs)]
            d_rows = [d_ref[i, pl.ds(at, 8), cols] for i in range(segs)]
            sums = [[] for _ in range(segs)]
            for u in reversed(range(8)):
                following = []
                for i, grad in enumerate(grads):
                    d_row = d_rows[i][u : u + 1]
                    grad = grad * (decay * next_ref[i, at + u]) + eta * d_row
                    before = before_ref[i, at + u, :, cols]
                    kept = kept + d_row * before
                    decayed = decayed + grad * before
                    fed = fed + grad * rows[i][u : u + 1]
                    sums[i].insert(0, jnp.sum(feed * grad, axis=0, keepdims=True))
                    following.append(grad)
                grads = tuple(following)
            for i in range(segs):
                grad_ref[i, pl.ds(at, 8), cols] = jnp.concatenate(sums[i], axis=0) + omega * d_rows[i]
            return grads, kept, decayed, fed

        zero = jnp.zeros(decay.shape, F32)
        _, kept, decayed, fed = lax.fori_loop(0, length // 8, eight, (tuple(entering), zero, zero, zero))
        alpha, delta = alpha_ref[:, cols], delta_ref[:, cols]
        made = (
            alpha * fed,
            alpha * (1.0 - alpha) * (beta_ref[:, cols] * fed - delta * decayed),
            -delta * (1.0 - delta) * alpha * decayed,
            decay * kept + feed * omega_grad_ref[:, cols],
        )
        for i, gradient in enumerate(made):
            rates_ref[i * n_heads : (i + 1) * n_heads, cols] = gradient.astype(BF16)


def ema_fourth(
    place, slots, passes, keep, keep_next, d_smoothed, normed, enter, heads_grad, long_decay, decay, feed, eta, omega,
    alpha, delta, beta, omega_grad,
):
    segs, length, width = normed.shape
    return pl.pallas_call(
        fourth_kernel,
        out_shape=(
            jax.ShapeDtypeStruct(normed.shape, F32),
            jax.ShapeDtypeStruct((4 * decay.shape[0], width), BF16),
        ),
        in_specs=[SMEM()] * 5 + [VMEM()] * 13,
        out_specs=(VMEM(),) * 2,
        scratch_shapes=[pltpu.VMEM((segs, length, *decay.shape), F32)],
        compiler_params=pltpu.CompilerParams(vmem_limit_bytes=24 * MIB),
        cost_estimate=BRIEF,
        name="ema_fourth",
    )(
        place, slots, passes, keep, keep_next, d_smoothed, normed, enter, heads_grad, long_decay, decay, feed, eta, omega,
        alpha, delta, beta, omega_grad,
    )


def values_kernel(x_ref, gain_ref, w_ref, normed_ref, values_ref, slope_ref):
    segs, length, width = x_ref.shape
    x = x_ref[...].astype(F32).reshape(segs * length, width)
    normed = (norm_parts(x)[0] * gain_ref[...]).astype(BF16)
    normed_ref[...] = normed
    wide = w_ref.shape[1]
    chunk = wide // 3
    for c in range(0, wide, chunk):
        pre = dot(normed, w_ref[:, c : c + chunk], ((1,), (0,)))
        gate = logistic(pre)
        value = pre * gate
        values_ref[:, c : c + chunk] = value.astype(BF16)
        slope_ref[:, c : c + chunk] = (gate + value * (1.0 - gate)).astype(BF16)


def row_values(x, gain, w_value):
    segs, length, width = x.shape
    wide = w_value.shape[1]
    rows = 2 * length
    count = segs * length
    return pl.pallas_call(
        values_kernel,
        grid=(segs // 2,),
        out_shape=(
            jax.ShapeDtypeStruct((count, width), BF16),
            jax.ShapeDtypeStruct((count, wide), BF16),
            jax.ShapeDtypeStruct((count, wide), BF16),
        ),
        in_specs=[pl.BlockSpec((2, length, width), lambda b: (b, 0, 0)), whole(1, width), whole(width, wide)],
        out_specs=(
            pl.BlockSpec((rows, width), lambda b: (b, 0)),
            pl.BlockSpec((rows, wide), lambda b: (b, 0)),
            pl.BlockSpec((rows, wide), lambda b: (b, 0)),
        ),
        compiler_params=pltpu.CompilerParams(vmem_limit_bytes=16 * MIB),
        cost_estimate=BRIEF,
        name="row_values",
    )(x, gain, w_value)


def values_back_kernel(probs_ref, d_ref, slope_ref, w_ref, pre_ref, near_ref, far_ref):
    wide = d_ref.shape[1]
    chunk = wide // 3
    total = jnp.zeros(near_ref.shape, F32)
    for c in range(0, wide, chunk):
        cols = slice(c, c + chunk)
        d_values = dot(probs_ref[...], d_ref[:, cols], ((0,), (0,)))
        pre = (d_values * slope_ref[:, cols].astype(F32)).astype(BF16)
        pre_ref[:, cols] = pre
        total = total + dot(pre, w_ref[:, cols], ((1,), (1,)))
    step, steps = pl.program_id(0), pl.num_programs(0)

    @pl.when(step < steps // 2)
    def _():
        near_ref[...] = total.astype(BF16)

    @pl.when(step >= steps // 2)
    def _():
        far_ref[...] = total.astype(BF16)


def values_back(probs, d_attended, slope, w_value):
    count, every = probs.shape
    width, wide = w_value.shape
    rows = 256
    half = every // rows // 2
    return pl.pallas_call(
        values_back_kernel,
        grid=(every // rows,),
        out_shape=(
            jax.ShapeDtypeStruct((every, wide), BF16),
            jax.ShapeDtypeStruct((every // 2, width), BF16),
            jax.ShapeDtypeStruct((every // 2, width), BF16),
        ),
        in_specs=[
            pl.BlockSpec((count, rows), lambda b: (0, b)),
            whole(count, wide),
            pl.BlockSpec((rows, wide), lambda b: (b, 0)),
            whole(width, wide),
        ],
        out_specs=(
            pl.BlockSpec((rows, wide), lambda b: (b, 0)),
            pl.BlockSpec((rows, width), lambda b: (jnp.minimum(b, half - 1), 0)),
            pl.BlockSpec((rows, width), lambda b: (jnp.maximum(b - half, 0), 0)),
        ),
        compiler_params=pltpu.CompilerParams(vmem_limit_bytes=16 * MIB),
        cost_estimate=BRIEF,
        name="values_back",
    )(probs, d_attended, slope, w_value)


def attend_kernel(
    scale, at_ref, doc_ref, every_at_ref, every_doc_ref, q_ref, k_ref, v_ref, reset_ref,
    weight_ref, probs_ref, inverse_ref, attended_ref, gated_ref,
):
    count, every = probs_ref.shape
    chunk = 256

    @pl.when(pl.program_id(0) == 0)
    def _():
        def scores(j, highest):
            keys = pl.ds(pl.multiple_of(j * chunk, chunk), chunk)
            raw = dot(q_ref[...], k_ref[keys, :], ((1,), (1,))) * scale
            visible = (every_doc_ref[:, keys] == doc_ref[...]) & (every_at_ref[:, keys] <= at_ref[...])
            raw = jnp.where(visible, raw, MASKED_SCORE)
            weight_ref[:, keys] = raw
            return jnp.maximum(highest, jnp.maximum(raw[:, :128], raw[:, 128:]))

        highest = lax.fori_loop(0, every // chunk, scores, jnp.full((count, 128), MASKED_SCORE, F32))
        highest = jnp.max(highest, axis=1, keepdims=True)

        def weights(j, total):
            keys = pl.ds(pl.multiple_of(j * chunk, chunk), chunk)
            weight = jnp.exp(weight_ref[:, keys] - highest)
            weight_ref[:, keys] = weight
            return total + (weight[:, :128] + weight[:, 128:])

        total = lax.fori_loop(0, every // chunk, weights, jnp.zeros((count, 128), F32))
        inverse = 1.0 / jnp.sum(total, axis=1, keepdims=True)
        inverse_ref[...] = inverse

        def rounded(j, nothing):
            keys = pl.ds(pl.multiple_of(j * chunk, chunk), chunk)
            probs_ref[:, keys] = (weight_ref[:, keys] * inverse).astype(BF16)
            return nothing

        lax.fori_loop(0, every // chunk, rounded, 0)

    attended = dot(probs_ref[...], v_ref[...], ((1,), (0,)))
    attended_ref[...] = attended
    reset = reset_ref[...]
    gated_ref[...] = (reset * logistic(reset) * attended).astype(BF16)


def attend(scale, at, doc, every_at, every_doc, queries, keys, values, reset_pre):
    count, zdim = queries.shape
    every, wide = values.shape
    chunk = 256
    columns = pl.BlockSpec((count, chunk), lambda c: (0, c))
    return pl.pallas_call(
        functools.partial(attend_kernel, scale),
        grid=(wide // chunk,),
        out_shape=(
            jax.ShapeDtypeStruct((count, every), F32),
            jax.ShapeDtypeStruct((count, every), BF16),
            jax.ShapeDtypeStruct((count, 1), F32),
            jax.ShapeDtypeStruct((count, wide), F32),
            jax.ShapeDtypeStruct((count, wide), BF16),
        ),
        in_specs=[
            whole(count, 1), whole(count, 1), whole(1, every), whole(1, every),
            whole(count, zdim), whole(every, zdim), pl.BlockSpec((every, chunk), lambda c: (0, c)), columns,
        ],
        out_specs=(whole(count, every), whole(count, every), whole(count, 1), columns, columns),
        compiler_params=pltpu.CompilerParams(vmem_limit_bytes=(6 + every * 7 // 2048) * MIB),
        cost_estimate=BRIEF,
        name="attend",
    )(at, doc, every_at, every_doc, queries, keys, values, reset_pre)


def middle_kernel(
    gated_ref, attended_ref, reset_ref, update_ref, cand_ref, x_ref, cot_ref, out_w_ref, up_w_ref, down_w_ref, gain_ref,
    output_ref, in_ref, hidden_ref, d_up_ref, d_tail_ref, skip_ref, gain_grad_ref, d_attended_ref, delta_ref,
    after_ref, sum_ref, normed_ref, back_ref,
):
    count, width = x_ref.shape
    wide = gated_ref.shape[1]
    chunk = 256
    for c in range(0, width, chunk):
        cols = slice(c, c + chunk)
        cand = cand_ref[:, cols] + dot(gated_ref[...], out_w_ref[:, cols], ((1,), (0,)))
        sum_ref[:, cols] = cand
        x = x_ref[:, cols].astype(F32)
        after_ref[:, cols] = x + logistic(update_ref[:, cols]) * (cand * logistic(cand) - x)
    gain = gain_ref[...]
    tall = 64
    for r in range(0, count, tall):
        rows = slice(r, r + tall)
        normed = norm_parts(after_ref[rows, :])[0]
        normed_ref[rows, :] = normed
        in_ref[rows, :] = (normed * gain).astype(BF16)
    for c in range(0, wide, chunk):
        cols = slice(c, c + chunk)
        up = dot(in_ref[...], up_w_ref[:, cols], ((1,), (0,)))
        gate = logistic(up)
        high = up * gate
        hidden_ref[:, cols] = high.astype(BF16)
        d_hidden = dot(cot_ref[...], down_w_ref[cols, :], ((1,), (1,)))
        d_up_ref[:, cols] = (d_hidden * (gate + high * (1.0 - gate))).astype(BF16)
    for c in range(0, width, chunk):
        cols = slice(c, c + chunk)
        result = after_ref[:, cols] + dot(hidden_ref[...], down_w_ref[:, cols], ((1,), (0,)))
        output_ref[:, cols] = result.astype(BF16)
        back_ref[:, cols] = dot(d_up_ref[...], up_w_ref[cols, :], ((1,), (1,)))
    gain_grad = jnp.zeros((1, width), F32)
    for r in range(0, count, tall):
        rows = slice(r, r + tall)
        back, normed, old = back_ref[rows, :], normed_ref[rows, :], after_ref[rows, :]
        inverse = norm_parts(old)[1]
        gain_grad = gain_grad + jnp.sum(back * normed, axis=0, keepdims=True)
        scaled = back * gain
        first = jnp.mean(scaled, axis=-1, keepdims=True)
        second = jnp.mean(scaled * normed, axis=-1, keepdims=True)
        d_after = cot_ref[rows, :].astype(F32) + inverse * (scaled - first - normed * second)
        update = logistic(update_ref[rows, :])
        cand = sum_ref[rows, :]
        gate = logistic(cand)
        high = cand * gate
        skip_ref[rows, :] = d_after * (1.0 - update)
        taken = d_after * update
        d_update = taken * (1.0 - update) * (high - x_ref[rows, :].astype(F32))
        d_tail_ref[rows, wide : wide + width] = d_update.astype(BF16)
        d_tail_ref[rows, wide + width :] = (taken * (gate + high * (1.0 - gate))).astype(BF16)
    gain_grad_ref[...] = gain_grad
    delta = jnp.zeros((count, 1), F32)
    for c in range(0, wide, chunk):
        cols = slice(c, c + chunk)
        d_gated = dot(d_tail_ref[:, wide + width :], out_w_ref[cols, :], ((1,), (1,)))
        attended = attended_ref[:, cols]
        reset = reset_ref[:, cols]
        gate = logistic(reset)
        high = reset * gate
        d_tail_ref[:, cols] = (d_gated * attended * (gate + high * (1.0 - gate))).astype(BF16)
        d_attended = (d_gated * high).astype(BF16)
        d_attended_ref[:, cols] = d_attended
        delta = delta + jnp.sum(d_attended.astype(F32) * attended, axis=1, keepdims=True)
    delta_ref[...] = delta


def middle(gated, attended, reset_pre, update_pre, cand_part, x, cot, w_out, w_up, w_down, gain):
    count, width = x.shape
    wide = gated.shape[1]

    def low(*shape):
        return jax.ShapeDtypeStruct(shape, BF16)

    def full(*shape):
        return jax.ShapeDtypeStruct(shape, F32)

    return pl.pallas_call(
        middle_kernel,
        out_shape=(
            low(count, width), low(count, width), low(count, wide), low(count, wide), low(count, wide + 2 * width),
            full(count, width), full(1, width), low(count, wide), full(count, 1),
        ),
        in_specs=[VMEM()] * 11,
        out_specs=(VMEM(),) * 9,
        scratch_shapes=[pltpu.VMEM((count, width), F32)] * 4,
        compiler_params=pltpu.CompilerParams(vmem_limit_bytes=28 * MIB),
        cost_estimate=BRIEF,
        name="middle",
    )(gated, attended, reset_pre, update_pre, cand_part, x, cot, w_out, w_up, w_down, gain)


def scores_back_kernel(scale, weight_ref, inverse_ref, delta_ref, d_ref, v_ref, q_ref, k_ref, near_ref, far_ref, dq_ref):
    step, steps = pl.program_id(0), pl.num_programs(0)
    d_probs = dot(d_ref[...], v_ref[...], ((1,), (1,)))
    probs = weight_ref[...] * inverse_ref[...]
    d_score = (probs * (d_probs - delta_ref[...]) * scale).astype(BF16)
    d_keys = dot(d_score, q_ref[...], ((0,), (0,))).astype(BF16)

    @pl.when(step < steps // 2)
    def _():
        near_ref[...] = d_keys

    @pl.when(step >= steps // 2)
    def _():
        far_ref[...] = d_keys

    d_queries = dot(d_score, k_ref[...], ((1,), (0,)))

    @pl.when(step == 0)
    def _():
        dq_ref[...] = d_queries

    @pl.when(step > 0)
    def _():
        dq_ref[...] += d_queries


def scores_back(scale, weight, inverse, delta, d_attended, values, queries, keys):
    count, every = weight.shape
    zdim, wide = queries.shape[1], values.shape[1]
    rows = 256
    half = every // rows // 2
    return pl.pallas_call(
        functools.partial(scores_back_kernel, scale),
        grid=(every // rows,),
        out_shape=(
            jax.ShapeDtypeStruct((every // 2, zdim), BF16),
            jax.ShapeDtypeStruct((every // 2, zdim), BF16),
            jax.ShapeDtypeStruct((count, zdim), F32),
        ),
        in_specs=[
            pl.BlockSpec((count, rows), lambda b: (0, b)), whole(count, 1), whole(count, 1), whole(count, wide),
            pl.BlockSpec((rows, wide), lambda b: (b, 0)), whole(count, zdim), pl.BlockSpec((rows, zdim), lambda b: (b, 0)),
        ],
        out_specs=(
            pl.BlockSpec((rows, zdim), lambda b: (jnp.minimum(b, half - 1), 0)),
            pl.BlockSpec((rows, zdim), lambda b: (jnp.maximum(b - half, 0), 0)),
            whole(count, zdim),
        ),
        compiler_params=pltpu.CompilerParams(vmem_limit_bytes=10 * MIB),
        cost_estimate=BRIEF,
        name="scores_back",
    )(weight, inverse, delta, d_attended, values, queries, keys)


def third_kernel(
    next_ref, dq_ref, z_ref, query_ref, key_ref, d_tail_ref, w_ref, mixed_ref, smoothed_ref, normed_ref, decay_ref,
    eta_ref, *refs
):
    *part_refs, dz_ref, zw_ref, d_ref, head_ref, omega_ref, small_ref = refs
    segs, length, width = d_ref.shape
    zdim = dq_ref.shape[1]
    d_keys = sum(part_ref[...].astype(F32) for part_ref in part_refs)
    z, d_queries = z_ref[...], dq_ref[...]
    gate = logistic(z)
    shared = z * gate
    small_ref[0:1, :] = jnp.sum(d_queries * shared, axis=0, keepdims=True)
    small_ref[1:2, :] = jnp.sum(d_queries, axis=0, keepdims=True)
    small_ref[2:3, :] = jnp.sum(d_keys * shared, axis=0, keepdims=True)
    d_shared = d_queries * query_ref[...] + d_keys * key_ref[...]
    dz_ref[...] = (d_shared * (gate + shared * (1.0 - gate))).astype(BF16)
    zw_ref[...] = dot(dz_ref[...], mixed_ref[...], ((0,), (0,))).astype(BF16)
    part = 256
    for c in range(0, width, part):
        cols = slice(c, c + part)
        back = dot(dz_ref[...], w_ref[cols, :zdim], ((1,), (1,))) + dot(d_tail_ref[...], w_ref[cols, zdim:], ((1,), (1,)))
        omega = jnp.zeros((1, part), F32)
        for i in range(segs):
            smoothed = smoothed_ref[i, :, cols]
            gate = logistic(smoothed)
            slope = gate * (1.0 + smoothed * (1.0 - gate))
            d_smoothed = back[i * length : (i + 1) * length] * slope
            d_ref[i, :, cols] = d_smoothed
            omega = omega + jnp.sum(d_smoothed * normed_ref[i, :, cols], axis=0, keepdims=True)
        omega_ref[:, cols] = omega
    part = width // 2
    for c in range(0, width, part):
        cols = slice(c, c + part)
        decay, eta = decay_ref[:, cols], eta_ref[:, cols]

        def eight(block, grads):
            at = pl.multiple_of(length - 8 - block * 8, 8)
            rows = [d_ref[i, pl.ds(at, 8), cols] for i in range(segs)]
            for u in reversed(range(8)):
                grads = tuple(
                    grad * (decay * next_ref[i, at + u]) + eta * rows[i][u : u + 1]
                    for i, grad in enumerate(grads)
                )
            return grads

        zero = jnp.zeros(decay.shape, F32)
        grads = lax.fori_loop(0, length // 8, eight, (zero,) * segs)
        for i in range(segs):
            head_ref[i, :, cols] = grads[i]


def ema_third(
    keep_next, d_queries, z_pre, query_gain, key_gain, d_tail, w_mix, mixed_in, smoothed, normed, decay, eta, *parts
):
    segs, length, width = normed.shape
    count, zdim = z_pre.shape
    return pl.pallas_call(
        third_kernel,
        out_shape=(
            jax.ShapeDtypeStruct((count, zdim), BF16),
            jax.ShapeDtypeStruct((zdim, width), BF16),
            jax.ShapeDtypeStruct(normed.shape, F32),
            jax.ShapeDtypeStruct((segs, *decay.shape), F32),
            jax.ShapeDtypeStruct((1, width), F32),
            jax.ShapeDtypeStruct((3, zdim), F32),
        ),
        in_specs=[SMEM()] + [VMEM()] * (11 + len(parts)),
        out_specs=(VMEM(),) * 6,
        compiler_params=pltpu.CompilerParams(vmem_limit_bytes=20 * MIB),
        cost_estimate=BRIEF,
        name="ema_third",
    )(keep_next, d_queries, z_pre, query_gain, key_gain, d_tail, w_mix, mixed_in, smoothed, normed, decay, eta, *parts)


def half_kernel(halved, half_ref, slot_ref, *refs):
    *refs, low_ref, high_ref = refs
    half = low_ref.shape[0]
    blocks = 2 * half
    at = 0
    for i, kind in enumerate(halved):
        left_ref, right_ref = refs[2 * i], refs[2 * i + 1]
        (count, tall), wide = left_ref.shape, right_ref.shape[1]
        piece = min(count, 2048)
        own_left = slice(None)
        if kind == "left":
            tall //= 2
            own_left = pl.ds(pl.multiple_of(half_ref[0] * tall, 128), tall)
        else:
            wide //= 2
        rows = tall // blocks
        chunk = 384
        for c in range(0, wide, chunk):
            own_right = slice(c, c + chunk)
            if kind == "right":
                own_right = pl.ds(pl.multiple_of(half_ref[0] * wide + c, 128), chunk)
            part = sum(
                dot(left_ref[k : k + piece, own_left], right_ref[k : k + piece, own_right], ((0,), (0,)))
                for k in range(0, count, piece)
            )
            for b in range(blocks):
                slot = slot_ref[b]
                own = part[b * rows : (b + 1) * rows].astype(BF16)

                @pl.when(slot < half)
                def _():
                    low_ref[slot, at : at + rows, c : c + chunk] = own

                @pl.when(slot >= half)
                def _():
                    high_ref[slot - half, at : at + rows, c : c + chunk] = own

        at += rows


def grad_half(half, slots, halved, *pairs):
    blocks = slots.shape[0]
    rows, held = 0, 0
    for i, kind in enumerate(halved):
        left, right = pairs[2 * i], pairs[2 * i + 1]
        rows += left.shape[1] // (2 if kind == "left" else 1) // blocks
        held += 2 * (left.size + right.size) + left.shape[1] * right.shape[1]
        wide = right.shape[1] // (1 if kind == "left" else 2)
    return pl.pallas_call(
        functools.partial(half_kernel, halved),
        out_shape=(jax.ShapeDtypeStruct((blocks // 2, rows, wide), BF16),) * 2,
        in_specs=[SMEM()] * 2 + [VMEM()] * len(pairs),
        out_specs=(VMEM(),) * 2,
        compiler_params=pltpu.CompilerParams(vmem_limit_bytes=held + 8 * MIB),
        cost_estimate=BRIEF,
        name="grad_half",
    )(half, slots, *pairs)


def place_kernel(halved, lead, step, core_ref, slot_ref, near_ref, far_ref, near_other_ref, far_other_ref, *out_refs):
    half, _, wide = near_ref.shape
    core = core_ref[0]
    for b in range(step):
        slot = slot_ref[pl.program_id(0) * step + b]

        def put(own, other):
            at = 0
            for kind, out_ref in zip(halved, out_refs, strict=True):
                if kind == "right":
                    rows = out_ref.shape[1]
                    mine = pl.ds(pl.multiple_of(core * wide, 128), wide)
                    others = pl.ds(pl.multiple_of((1 - core) * wide, 128), wide)
                    out_ref[b, :, mine] = own[at : at + rows].astype(F32)
                    out_ref[b, :, others] = other[at : at + rows].astype(F32)
                else:
                    rows = out_ref.shape[2]
                    if lead:
                        out_ref[:, b, :, :lead] = jnp.zeros((2, rows, lead), F32)
                    out_ref[core, b, :, lead:] = own[at : at + rows].astype(F32)
                    out_ref[1 - core, b, :, lead:] = other[at : at + rows].astype(F32)
                at += rows

        @pl.when(slot < half)
        def _():
            put(near_ref[slot], near_other_ref[slot])

        @pl.when(slot >= half)
        def _():
            put(far_ref[slot - half], far_other_ref[slot - half])


def put_in_place(core, slots, halved, talls, lead, near, far, near_other, far_other):
    half, rows, wide = near.shape
    blocks = 2 * half
    step = 2
    shapes, specs = [], []
    for kind, tall in zip(halved, talls, strict=True):
        if kind != "left":
            each = tall // blocks
            shapes.append(jax.ShapeDtypeStruct((blocks, each, 2 * wide), F32))
            specs.append(pl.BlockSpec((step, each, 2 * wide), lambda b: (b, 0, 0)))
        else:
            each = tall // 2 // blocks
            shapes.append(jax.ShapeDtypeStruct((2, blocks, each, lead + wide), F32))
            specs.append(pl.BlockSpec((2, step, each, lead + wide), lambda b: (0, b, 0, 0)))
    outs = pl.pallas_call(
        functools.partial(place_kernel, halved, lead, step),
        grid=(blocks // step,),
        out_shape=shapes,
        in_specs=[SMEM()] * 2 + [whole(half, rows, wide)] * 4,
        out_specs=specs,
        compiler_params=pltpu.CompilerParams(vmem_limit_bytes=20 * MIB),
        cost_estimate=BRIEF,
        name="put_in_place",
    )(core, slots, near, far, near_other, far_other)
    return [out.reshape(tall, -1) for out, tall in zip(outs, talls, strict=True)]


def after(value, *others):
    return lax.optimization_barrier((value, *others))[0]


def added(one, two):
    return (one.astype(F32) + two.astype(F32)).astype(one.dtype)


CORES = [(0, 1), (1, 0)]


def swapped(part):
    return lax.ppermute(part, "core", CORES)


def across(part, bit):
    chips = lax.axis_size("g") * lax.axis_size("s")
    return lax.ppermute(part, ("g", "s"), [(i, i ^ (1 << bit)) for i in range(chips)])


class Lane:
    def __init__(self, order, back, halved):
        chips = lax.axis_size("g") * lax.axis_size("s")
        bits = chips.bit_length() - 1
        order = list(order) + [bit for bit in range(bits) if bit not in order]
        self.cut, self.rest, self.halved = order[:3], order[3:], halved
        chip = lax.axis_index(("g", "s"))
        self.core = lax.axis_index("core").reshape(1)
        block = jnp.arange(1 << len(self.cut), dtype=jnp.int32)
        count = len(self.cut)
        self.slots = block ^ sum(((chip >> bit) & 1) << (count - 1 - t) for t, bit in enumerate(self.cut))
        self.back = [bit for bit in back if bit in self.cut]
        self.back_slots = sum(
            (((block >> (count - 1 - t)) ^ (chip >> bit)) & 1) << self.back.index(bit) for t, bit in enumerate(self.cut)
        )

    def theirs(self, *pairs):
        self.talls = [left.shape[1] for left in pairs[::2]]
        low, high = grad_half(1 - self.core, self.slots, self.halved, *pairs)
        self.received, self.received_low = swapped(high), swapped(low)
        return high

    def mine(self, *pairs):
        self.low, self.kept = grad_half(self.core, self.slots, self.halved, *pairs)
        self.turn = 0
        return self.kept

    def more(self):
        return self.turn < 2 * len(self.cut) + len(self.rest)

    def near_end(self):
        return self.turn >= 2 * len(self.cut) + len(self.rest) - 1

    def step(self, *others):
        received = after(self.received, *others)
        cut, rest = self.cut, self.rest
        doubled = self.turn - len(cut) - len(rest)
        if self.turn == 0:
            self.sent = added(self.kept, received)
            self.kept = added(self.low, after(self.received_low, self.sent))
            bit = cut[0]
        elif self.turn < len(cut):
            half = self.kept.shape[0] // 2
            self.sent = added(self.kept[half:], received[half:])
            self.kept = added(self.kept[:half], received[:half])
            bit = cut[self.turn]
        elif doubled < 0:
            self.sent = self.kept = added(self.kept, received)
            bit = rest[self.turn - len(cut)]
        elif doubled == 0:
            self.sent = added(self.kept, received)
            bit = self.back[0]
        else:
            self.sent = jnp.concatenate([self.sent, received])
            bit = self.back[doubled]
        self.received = across(self.sent, bit)
        self.turn += 1
        return self.sent

    def arrive(self, *others):
        self.received = after(self.received, *others)
        self.others = swapped(after(self.sent, self.received)), swapped(self.received)
        return self.received

    def end(self, last, lead=0):
        return put_in_place(
            self.core, self.back_slots, self.halved, self.talls, lead,
            self.sent, self.received, *after(self.others, last),
        )


def local(
    tokens,
    cotangent,
    doc_lengths,
    attn_gain,
    ema_beta,
    alpha_raw,
    delta_raw,
    ema_eta,
    ema_omega,
    w_value,
    w_mix,
    query_gain,
    query_bias,
    key_gain,
    w_out,
    ffn_gain,
    w_up,
    w_down,
):
    held, seg_len, width = tokens.shape
    planes, around = lax.axis_size("g"), lax.axis_size("s")
    g, s, core = lax.axis_index("g"), lax.axis_index("s"), lax.axis_index("core")
    odd = g % 2
    count = 2 * seg_len
    zdim = query_gain.shape[0]
    vdim = w_value.shape[1]
    scale_factor = zdim ** (-0.5)

    def number(z, x, c):
        return (z * around + x) * 2 + c

    routes = [
        [
            (number(z, x, c), number(2 * c + ((z % 2) ^ a), x, z // 2))
            for z in range(planes)
            for x in range(around)
            for c in range(2)
        ]
        for a in range(2)
    ]

    def to_planes(rows):
        return jnp.concatenate(
            [
                lax.ppermute(lax.dynamic_slice_in_dim(rows, odd ^ a, 1, 0), EVERY, routes[a])
                for a in range(2)
            ]
        )

    def from_planes(segs):
        return [
            lax.ppermute(segs[a : a + 1], EVERY, [(b, a_) for a_, b in routes[a]])
            for a in range(2)
        ]

    def in_order(back):
        return jnp.concatenate(
            [jnp.where(odd == 0, back[0], back[1]), jnp.where(odd == 0, back[1], back[0])]
        )

    def nearby(part, k):
        return lax.ppermute(part, "s", [(i, i ^ k) for i in range(around)])

    def gathered_near(part):
        return jnp.concatenate([part] + [nearby(part, k) for k in range(1, around)])

    def gathered(part):
        near = gathered_near(part)
        return jnp.concatenate([near, swapped(near)])

    hops = range(around.bit_length() - 1)

    def hop_gather(part, hop):
        return jnp.concatenate([part, nearby(part, 1 << hop)])

    def hop_send(parts, hop):
        half = parts.shape[0] // 2
        return parts[:half], nearby(parts[half:], 1 << hop)

    def scattered_near(parts, received):
        mine = added(parts, received).reshape(around, parts.shape[0] // around, *parts.shape[1:])
        return mine, [nearby(mine[k], k) for k in range(1, around)]

    def scattered_sum(mine, received):
        total = mine[0].astype(F32)
        for part in received:
            total = total + part.astype(F32)
        return total

    x_rows = to_planes(tokens)

    other = lax.ppermute(doc_lengths, "core", [(0, 1), (1, 0)])
    lengths = jnp.where(g // 2 == core, doc_lengths[odd], other[odd])
    docs = lengths.shape[0]
    before_it = jnp.arange(docs)[:, None] > jnp.arange(docs)[None, :]
    starts = jnp.sum(jnp.where(before_it, lengths[None, :], 0), axis=1)

    def doc_of(positions):
        return jnp.sum((starts[:, None] <= positions[None, :]).astype(jnp.int32), axis=0) - 1

    def kept_at(positions):
        return 1.0 - jnp.any(starts[:, None] == positions[None, :], axis=0).astype(F32)

    def blocks_of(s_of, core_of):
        return [(2 * core_of + (odd ^ i)) * around + s_of for i in range(2)]

    place = jnp.stack(blocks_of(s, core))
    order = jnp.stack(
        [block for c in range(2) for k in range(around) for block in blocks_of(s ^ k, core ^ c)]
    )
    n_segs = order.shape[0]
    block = jnp.arange(n_segs, dtype=jnp.int32)
    other_core = (block // around // 2) ^ core
    near_slots = (other_core * around + ((block % around) ^ s)) * 2 + ((block // around % 2) ^ odd)
    within = jnp.arange(seg_len, dtype=jnp.int32)
    local_pos = (place[:, None] * seg_len + within).reshape(-1)
    every_pos = (order[:, None] * seg_len + within).reshape(-1)
    keep = kept_at(local_pos).reshape(2, seg_len)
    keep_next = kept_at(local_pos + 1).reshape(2, seg_len)
    row_keep = kept_at(jnp.arange(n_segs * seg_len + 1, dtype=jnp.int32))
    passes = jnp.min(row_keep[:-1].reshape(n_segs, seg_len), axis=1)
    passes_back = jnp.min(row_keep[1:].reshape(n_segs, seg_len), axis=1)

    ema_alpha = jax.nn.sigmoid(alpha_raw)
    ema_delta = jax.nn.sigmoid(delta_raw)
    decay = 1.0 - ema_alpha * ema_delta
    feed_gain = ema_alpha * ema_beta
    long_decay = decay
    reach = 1
    while reach < seg_len:
        long_decay = long_decay * long_decay
        reach *= 2
    gain_row, omega_row = attn_gain[None], ema_omega[None]

    normed_rows, ends = ema_first(keep, x_rows, gain_row, decay, feed_gain)
    near_ends = gathered_near(ends)
    every_end = jnp.concatenate([near_ends, swapped(near_ends)])
    every_x = gathered(after(x_rows, near_ends))
    cot_rows = to_planes(after(cotangent, near_ends))
    smoothed, mixed_in, states_enter = ema_second(
        place, near_slots, passes, keep, normed_rows, every_end, long_decay, decay, feed_gain, ema_eta, omega_row
    )
    mixed_in = mixed_in.reshape(count, width)

    z_pre = dot(mixed_in, w_mix[:, :zdim], ((1,), (0,)))
    shared = jax.nn.silu(z_pre)
    queries = (shared * query_gain + query_bias).astype(BF16)
    keys = (shared * key_gain).astype(BF16)
    every_key = gathered(keys)
    every_normed, values, value_slope = row_values(after(every_x, keys), gain_row, w_value)
    mixed_here = after(mixed_in, keys)
    reset_pre = dot(mixed_here, w_mix[:, zdim : zdim + vdim], ((1,), (0,)))
    update_pre = dot(mixed_here, w_mix[:, zdim + vdim : zdim + vdim + width], ((1,), (0,)))
    cand_part = dot(mixed_here, w_mix[:, zdim + vdim + width :], ((1,), (0,)))

    inputs_x = x_rows.reshape(count, width)
    weight, probs_low, inverse, attended, gated = attend(
        scale_factor, local_pos[:, None], doc_of(local_pos)[:, None], every_pos[None], doc_of(every_pos)[None],
        queries, every_key, values, reset_pre,
    )
    cot_flat = cot_rows.reshape(count, width)
    result, ffn_in, hidden, d_up, d_tail, d_skip, grad_ffn_gain, d_attended, delta_row = middle(
        gated, attended, reset_pre, update_pre, cand_part, inputs_x, cot_flat, w_out, w_up, w_down, ffn_gain[None]
    )
    d_cand = d_tail[:, vdim + width :]

    one, two = Lane((2, 0, 1, 3), (2, 1, 0), ("left", "right")), Lane((1, 0, 2, 3), (0, 1, 2), ("right",))
    three, four = Lane((2, 1, 0, 3), (0, 2, 1), ("left",)), Lane((0, 1, 2, 3), (0, 1, 2), ("left",))

    def all_step(last, *lanes):
        for lane in lanes:
            if lane.more():
                last = lane.step(last)
        return last

    last = one.theirs(gated, d_cand, ffn_in, d_up)
    last = three.theirs(after(mixed_in, last), d_tail)
    keys_sums, keys_far, d_queries = scores_back(
        scale_factor, weight, inverse, after(delta_row, last), d_attended, values, queries, every_key
    )
    keys_swapped = swapped(keys_far)
    last = one.mine(gated, d_cand, after(ffn_in, d_queries), d_up)
    last = one.step(last)
    keys_sums = added(keys_sums, after(keys_swapped, last))
    last = keys_sums
    for hop in reversed(hops):
        keys_kept, keys_near = hop_send(keys_sums, hop)
        if hop == hops[-1]:
            last = three.mine(after(mixed_in, last), d_tail)
            last = three.step(last)
            last = four.theirs(hidden, after(cot_flat, last))
        if hop > 0:
            keys_sums = added(keys_kept, after(keys_near, last))
            last = keys_sums
    last = four.mine(hidden, after(cot_flat, last))
    last = four.step(last)
    d_value_pre, normed_near_part, normed_far = values_back(
        after(probs_low, last), d_attended, value_slope, w_value
    )
    d_z_pre, grad_z, d_smoothed, grad_heads, grad_omega, grad_z_small = ema_third(
        keep_next, d_queries, z_pre, query_gain[None], key_gain[None], d_tail, w_mix, mixed_in, smoothed, normed_rows,
        decay, ema_eta, keys_kept, after(keys_near, d_value_pre),
    )
    heads = grad_heads
    for hop in hops:
        near = nearby(heads, 1 << hop)
        if hop == 0:
            last = two.theirs(every_normed, after(d_value_pre, heads))
            last = four.step(last)
            near = after(near, last)
        if hop == hops[-1]:
            last = two.mine(every_normed, after(d_value_pre, heads))
            near = after(near, last)
        heads = jnp.concatenate([heads, near])
    far = swapped(heads)
    normed_swapped = swapped(after(normed_far, heads))
    last = one.step(heads)
    last = two.step(last)
    every_head = jnp.concatenate([heads, after(far, last)])
    normed_sums = added(normed_near_part, after(normed_swapped, every_head))
    ema_normed, grad_rates = ema_fourth(
        place, near_slots, passes_back, keep, keep_next, d_smoothed, normed_rows, states_enter, every_head,
        long_decay, decay, feed_gain, ema_eta, omega_row, ema_alpha, ema_delta, ema_beta, grad_omega,
    )
    output = from_planes(after(result, grad_rates).reshape(2, seg_len, width))
    last = all_step(grad_rates, three, four, two, one)
    normed_kept, normed_near = hop_send(after(normed_sums, last, *output), hops[-1])
    output = in_order(output)
    last = all_step(last, three, four, two, one)
    for hop in reversed(hops[:-1]):
        last = added(normed_kept, after(normed_near, last))
        normed_kept, normed_near = hop_send(last, hop)
    last = all_step(last, three, four, two, one)
    d_normed = normed_kept.astype(F32) + after(normed_near, last).astype(F32)
    normed_one, inverse_one = norm_parts(inputs_x.astype(F32))
    d_norm_one, grad_attn_gain = norm_back(
        d_normed + ema_normed.reshape(count, width), normed_one, inverse_one, attn_gain
    )
    back = (d_skip + d_norm_one).astype(BF16)
    gains = jnp.concatenate(
        [
            grad_attn_gain[None],
            grad_omega,
            grad_ffn_gain,
            jnp.pad(grad_z_small.reshape(1, -1), ((0, 0), (0, width - 3 * zdim))),
            jnp.zeros((12, width), F32),
        ]
    )
    small = jnp.concatenate([grad_rates, gains.astype(BF16), grad_z])
    tall = small.shape[0] // 2
    small_far = lax.dynamic_slice_in_dim(small, (1 - core) * tall, tall)
    small_own = lax.dynamic_slice_in_dim(small, core * tall, tall)
    small, last = small_own, (small_far,)
    for bit in [None] + list(range((planes * around).bit_length() - 1)):
        small_near = swapped(small_far) if bit is None else across(after(small, *last), bit)
        last = all_step(small, *(lane for lane in (one, three, four, two) if not lane.near_end()))
        small = added(small, after(small_near, last))
        last = (small,)
        if bit == 0:
            sent_back = from_planes(after(back, small).reshape(2, seg_len, width))
        if bit == 1:
            last = (small, *sent_back)
    grad_tokens = in_order(sent_back).astype(F32)
    small_near = swapped(after(small, *last))
    last = small
    while not all(lane.near_end() for lane in (one, two, three, four)):
        last = all_step(last, *(lane for lane in (one, three, four, two) if not lane.near_end()))
    order_of_end = four, one, two, three
    last = all_step(last, *order_of_end)
    ended = {}
    for lane in order_of_end:
        last = lane.arrive(last)
    for lane in order_of_end:
        ended[lane] = lane.end(last, zdim if lane is three else 0)
        last = ended[lane][0]
    small_near = after(small_near, last)
    small = jnp.where(core == 0, jnp.concatenate([small, small_near]), jnp.concatenate([small_near, small]))
    small = small.astype(F32)
    (grad_wout, grad_up), (grad_value,), (grad_mix,), (grad_down,) = (ended[lane] for lane in (one, two, three, four))
    grad_mix = lax.dynamic_update_slice(grad_mix, small[-zdim:].T, (0, 0))
    n_heads = decay.shape[0]
    grad_beta, grad_alpha, grad_delta, grad_eta = (small[i * n_heads : (i + 1) * n_heads] for i in range(4))
    grad_attn_gain, grad_omega, grad_ffn_gain, last = (small[4 * n_heads + i] for i in range(4))
    grad_qgain, grad_qbias, grad_kgain = (last[i * zdim : (i + 1) * zdim] for i in range(3))
    return (
        output,
        grad_tokens,
        grad_attn_gain,
        grad_beta,
        grad_alpha,
        grad_delta,
        grad_eta,
        grad_omega,
        grad_value,
        grad_mix,
        grad_qgain,
        grad_qbias,
        grad_kgain,
        grad_wout,
        grad_ffn_gain,
        grad_up,
        grad_down,
    )


def solution(mesh):
    devices = mesh.devices
    finer = Mesh(devices.reshape(4, devices.shape[0] // 4, 2), EVERY)
    split = P("core", ("g", "s"), None)
    placed = (split, split, P("core", None)) + (P(),) * 15
    return jax.shard_map(
        local,
        mesh=finer,
        in_specs=placed,
        out_specs=(split, split) + (P(),) * 15,
        check_vma=False,
    )
```

```python
import functools

import jax
import jax.numpy as jnp
from jax import lax
from jax.experimental import pallas as pl
from jax.experimental.pallas import tpu as pltpu
from jax.sharding import Mesh
from jax.sharding import PartitionSpec as P

EPSILON = 1e-05
MASKED_SCORE = -1e30
BF16 = jnp.bfloat16
F32 = jnp.float32
EVERY = ("g", "s", "core")
MIB = 1024 * 1024
BRIEF = pl.CostEstimate(flops=1, bytes_accessed=1, transcendentals=0)


def logistic(inputs):
    return 0.5 * jnp.tanh(0.5 * inputs) + 0.5


def silu_slope(inputs):
    gate = logistic(inputs)
    return gate * (1.0 + inputs * (1.0 - gate))


def norm_parts(inputs):
    centred = inputs - jnp.mean(inputs, axis=-1, keepdims=True)
    inverse = lax.rsqrt(jnp.mean(centred * centred, axis=-1, keepdims=True) + EPSILON)
    return (centred * inverse, inverse)


def norm_back(upstream, normed, inverse, gain):
    scaled = upstream * gain
    first_mean = jnp.mean(scaled, axis=-1, keepdims=True)
    second_mean = jnp.mean(scaled * normed, axis=-1, keepdims=True)
    return (
        inverse * (scaled - first_mean - normed * second_mean),
        jnp.sum(upstream * normed, axis=0),
    )


def dot(left, right, contract):
    return lax.dot_general(left, right, (contract, ((), ())), preferred_element_type=F32)


SMEM = functools.partial(pl.BlockSpec, memory_space=pltpu.SMEM)


def in_hbm(value):
    return pltpu.with_memory_space_constraint(value, pltpu.HBM)


def whole(*shape):
    return pl.BlockSpec(shape, lambda *_: (0,) * len(shape))


def first_kernel(keep_ref, x_ref, gain_ref, decay_ref, feed_ref, normed_ref, last_ref):
    segs, length, width = x_ref.shape
    for i in range(segs):
        normed_ref[i] = norm_parts(x_ref[i].astype(F32))[0] * gain_ref[...]
    part = width // 2
    for c in range(0, width, part):
        cols = slice(c, c + part)
        decay, feed = decay_ref[:, cols], feed_ref[:, cols]

        def eight(block, states):
            at = pl.multiple_of(block * 8, 8)
            rows = [normed_ref[i, pl.ds(at, 8), cols] for i in range(segs)]
            for u in range(8):
                states = tuple(
                    state * (decay * keep_ref[i, at + u]) + feed * rows[i][u : u + 1]
                    for i, state in enumerate(states)
                )
            return states

        zero = jnp.zeros(decay.shape, F32)
        states = lax.fori_loop(0, length // 8, eight, (zero,) * segs)
        for i in range(segs):
            last_ref[i, :, cols] = states[i]


def ema_first(keep, x, gain, decay, feed):
    segs, length, width = x.shape
    return pl.pallas_call(
        first_kernel,
        out_shape=(
            jax.ShapeDtypeStruct(x.shape, F32),
            jax.ShapeDtypeStruct((segs, *decay.shape), F32),
        ),
        in_specs=[SMEM()] + [pl.BlockSpec(memory_space=pltpu.VMEM)] * 4,
        out_specs=(pl.BlockSpec(memory_space=pltpu.VMEM),) * 2,
        compiler_params=pltpu.CompilerParams(vmem_limit_bytes=8 * MIB),
        cost_estimate=BRIEF,
        name="ema_first",
    )(keep, x, gain, decay, feed)


def second_kernel(
    place_ref, slot_ref, pass_ref, keep_ref, normed_ref, ends_ref, long_ref, decay_ref, feed_ref, eta_ref, omega_ref,
    smoothed_ref, mixed_ref, enter_ref,
):
    segs, length, width = normed_ref.shape
    for i in range(segs):

        def hop(p, state):
            return state * (long_ref[...] * pass_ref[p]) + ends_ref[slot_ref[p]]

        enter_ref[i] = lax.fori_loop(0, place_ref[i], hop, jnp.zeros(decay_ref.shape, F32))

    part = width // 2
    for c in range(0, width, part):
        cols = slice(c, c + part)
        decay, feed, eta = decay_ref[:, cols], feed_ref[:, cols], eta_ref[:, cols]
        omega = omega_ref[:, cols]

        def eight(block, states):
            at = pl.multiple_of(block * 8, 8)
            rows = [normed_ref[i, pl.ds(at, 8), cols] for i in range(segs)]
            sums = [[] for _ in range(segs)]
            for u in range(8):
                following = []
                for i, state in enumerate(states):
                    state = state * (decay * keep_ref[i, at + u]) + feed * rows[i][u : u + 1]
                    sums[i].append(jnp.sum(eta * state, axis=0, keepdims=True))
                    following.append(state)
                states = tuple(following)
            for i in range(segs):
                smooth = jnp.concatenate(sums[i], axis=0) + omega * rows[i]
                smoothed_ref[i, pl.ds(at, 8), cols] = smooth
            return states

        lax.fori_loop(0, length // 8, eight, tuple(enter_ref[i, :, cols] for i in range(segs)))
    smoothed = smoothed_ref[...]
    mixed_ref[...] = (smoothed * logistic(smoothed)).astype(BF16)


VMEM = functools.partial(pl.BlockSpec, memory_space=pltpu.VMEM)


def ema_second(place, slots, passes, keep, normed, ends, long_decay, decay, feed, eta, omega):
    segs, length, width = normed.shape
    return pl.pallas_call(
        second_kernel,
        out_shape=(
            jax.ShapeDtypeStruct(normed.shape, F32),
            jax.ShapeDtypeStruct(normed.shape, BF16),
            jax.ShapeDtypeStruct((segs, *decay.shape), F32),
        ),
        in_specs=[SMEM()] * 4 + [VMEM()] * 7,
        out_specs=(VMEM(),) * 3,
        compiler_params=pltpu.CompilerParams(vmem_limit_bytes=12 * MIB),
        cost_estimate=BRIEF,
        name="ema_second",
    )(place, slots, passes, keep, normed, ends, long_decay, decay, feed, eta, omega)


def fourth_kernel(
    place_ref, slot_ref, pass_ref, keep_ref, next_ref, d_ref, normed_ref, enter_ref, heads_ref, long_ref,
    decay_ref, feed_ref, eta_ref, omega_ref, alpha_ref, delta_ref, beta_ref, omega_grad_ref, grad_ref, rates_ref, before_ref,
):
    segs, length, width = normed_ref.shape
    n_heads = decay_ref.shape[0]
    half = width // 2
    for c in range(0, width, half):
        cols = slice(c, c + half)
        decay, feed = decay_ref[:, cols], feed_ref[:, cols]

        def again(block, states):
            at = pl.multiple_of(block * 8, 8)
            rows = [normed_ref[i, pl.ds(at, 8), cols] for i in range(segs)]
            for u in range(8):
                following = []
                for i, state in enumerate(states):
                    state = state * keep_ref[i, at + u]
                    before_ref[i, at + u, :, cols] = state
                    following.append(state * decay + feed * rows[i][u : u + 1])
                states = tuple(following)
            return states

        lax.fori_loop(0, length // 8, again, tuple(enter_ref[i, :, cols] for i in range(segs)))

    count = slot_ref.shape[0]
    part = width // 3
    for c in range(0, width, part):
        cols = slice(c, c + part)
        decay, feed, eta = decay_ref[:, cols], feed_ref[:, cols], eta_ref[:, cols]
        omega = omega_ref[:, cols]
        entering = []
        for i in range(segs):

            def hop(back, grad):
                p = count - 1 - back
                return grad * (long_ref[:, cols] * pass_ref[p]) + heads_ref[slot_ref[p], :, cols]

            entering.append(lax.fori_loop(0, count - 1 - place_ref[i], hop, jnp.zeros(decay.shape, F32)))

        def eight(block, carried):
            grads, kept, decayed, fed = carried
            at = pl.multiple_of(length - 8 - block * 8, 8)
            rows = [normed_ref[i, pl.ds(at, 8), cols] for i in range(segs)]
            d_rows = [d_ref[i, pl.ds(at, 8), cols] for i in range(segs)]
            sums = [[] for _ in range(segs)]
            for u in reversed(range(8)):
                following = []
                for i, grad in enumerate(grads):
                    d_row = d_rows[i][u : u + 1]
                    grad = grad * (decay * next_ref[i, at + u]) + eta * d_row
                    before = before_ref[i, at + u, :, cols]
                    kept = kept + d_row * before
                    decayed = decayed + grad * before
                    fed = fed + grad * rows[i][u : u + 1]
                    sums[i].insert(0, jnp.sum(feed * grad, axis=0, keepdims=True))
                    following.append(grad)
                grads = tuple(following)
            for i in range(segs):
                grad_ref[i, pl.ds(at, 8), cols] = jnp.concatenate(sums[i], axis=0) + omega * d_rows[i]
            return grads, kept, decayed, fed

        zero = jnp.zeros(decay.shape, F32)
        _, kept, decayed, fed = lax.fori_loop(0, length // 8, eight, (tuple(entering), zero, zero, zero))
        alpha, delta = alpha_ref[:, cols], delta_ref[:, cols]
        made = (
            alpha * fed,
            alpha * (1.0 - alpha) * (beta_ref[:, cols] * fed - delta * decayed),
            -delta * (1.0 - delta) * alpha * decayed,
            decay * kept + feed * omega_grad_ref[:, cols],
        )
        for i, gradient in enumerate(made):
            rates_ref[i * n_heads : (i + 1) * n_heads, cols] = gradient.astype(BF16)


def ema_fourth(
    place, slots, passes, keep, keep_next, d_smoothed, normed, enter, heads_grad, long_decay, decay, feed, eta, omega,
    alpha, delta, beta, omega_grad,
):
    segs, length, width = normed.shape
    return pl.pallas_call(
        fourth_kernel,
        out_shape=(
            jax.ShapeDtypeStruct(normed.shape, F32),
            jax.ShapeDtypeStruct((4 * decay.shape[0], width), BF16),
        ),
        in_specs=[SMEM()] * 5 + [VMEM()] * 13,
        out_specs=(VMEM(),) * 2,
        scratch_shapes=[pltpu.VMEM((segs, length, *decay.shape), F32)],
        compiler_params=pltpu.CompilerParams(vmem_limit_bytes=24 * MIB),
        cost_estimate=BRIEF,
        name="ema_fourth",
    )(
        place, slots, passes, keep, keep_next, d_smoothed, normed, enter, heads_grad, long_decay, decay, feed, eta, omega,
        alpha, delta, beta, omega_grad,
    )


def values_kernel(x_ref, gain_ref, w_ref, normed_ref, values_ref, slope_ref):
    segs, length, width = x_ref.shape
    x = x_ref[...].astype(F32).reshape(segs * length, width)
    normed = (norm_parts(x)[0] * gain_ref[...]).astype(BF16)
    normed_ref[...] = normed
    wide = w_ref.shape[1]
    chunk = wide // 3
    for c in range(0, wide, chunk):
        pre = dot(normed, w_ref[:, c : c + chunk], ((1,), (0,)))
        gate = logistic(pre)
        value = pre * gate
        values_ref[:, c : c + chunk] = value.astype(BF16)
        slope_ref[:, c : c + chunk] = (gate + value * (1.0 - gate)).astype(BF16)


def row_values(x, gain, w_value):
    segs, length, width = x.shape
    wide = w_value.shape[1]
    rows = 2 * length
    count = segs * length
    return pl.pallas_call(
        values_kernel,
        grid=(segs // 2,),
        out_shape=(
            pltpu.HBM((count, width), BF16),
            jax.ShapeDtypeStruct((count, wide), BF16),
            pltpu.HBM((count, wide), BF16),
        ),
        in_specs=[pl.BlockSpec((2, length, width), lambda b: (b, 0, 0)), whole(1, width), whole(width, wide)],
        out_specs=(
            pl.BlockSpec((rows, width), lambda b: (b, 0)),
            pl.BlockSpec((rows, wide), lambda b: (b, 0)),
            pl.BlockSpec((rows, wide), lambda b: (b, 0)),
        ),
        compiler_params=pltpu.CompilerParams(vmem_limit_bytes=16 * MIB),
        cost_estimate=BRIEF,
        name="row_values",
    )(x, gain, w_value)


def values_back_kernel(probs_ref, d_ref, slope_ref, w_ref, pre_ref, near_ref, far_ref):
    wide = d_ref.shape[1]
    chunk = wide // 3
    total = jnp.zeros(near_ref.shape, F32)
    for c in range(0, wide, chunk):
        cols = slice(c, c + chunk)
        d_values = dot(probs_ref[...], d_ref[:, cols], ((0,), (0,)))
        pre = (d_values * slope_ref[:, cols].astype(F32)).astype(BF16)
        pre_ref[:, cols] = pre
        total = total + dot(pre, w_ref[:, cols], ((1,), (1,)))
    step, steps = pl.program_id(0), pl.num_programs(0)

    @pl.when(step < steps // 2)
    def _():
        near_ref[...] = total.astype(BF16)

    @pl.when(step >= steps // 2)
    def _():
        far_ref[...] = total.astype(BF16)


def values_back(probs, d_attended, slope, w_value):
    count, every = probs.shape
    width, wide = w_value.shape
    rows = 256
    half = every // rows // 2
    return pl.pallas_call(
        values_back_kernel,
        grid=(every // rows,),
        out_shape=(
            jax.ShapeDtypeStruct((every, wide), BF16),
            jax.ShapeDtypeStruct((every // 2, width), BF16),
            jax.ShapeDtypeStruct((every // 2, width), BF16),
        ),
        in_specs=[
            pl.BlockSpec((count, rows), lambda b: (0, b)),
            whole(count, wide),
            pl.BlockSpec((rows, wide), lambda b: (b, 0)),
            whole(width, wide),
        ],
        out_specs=(
            pl.BlockSpec((rows, wide), lambda b: (b, 0)),
            pl.BlockSpec((rows, width), lambda b: (jnp.minimum(b, half - 1), 0)),
            pl.BlockSpec((rows, width), lambda b: (jnp.maximum(b - half, 0), 0)),
        ),
        compiler_params=pltpu.CompilerParams(vmem_limit_bytes=16 * MIB),
        cost_estimate=BRIEF,
        name="values_back",
    )(in_hbm(probs), d_attended, in_hbm(slope), w_value)


def attend_kernel(
    scale, at_ref, doc_ref, every_at_ref, every_doc_ref, q_ref, k_ref, v_ref, reset_ref,
    weight_ref, probs_ref, inverse_ref, attended_ref, gated_ref,
):
    count, every = probs_ref.shape
    chunk = 256

    @pl.when(pl.program_id(0) == 0)
    def _():
        def scores(j, highest):
            keys = pl.ds(pl.multiple_of(j * chunk, chunk), chunk)
            raw = dot(q_ref[...], k_ref[keys, :], ((1,), (1,))) * scale
            visible = (every_doc_ref[:, keys] == doc_ref[...]) & (every_at_ref[:, keys] <= at_ref[...])
            raw = jnp.where(visible, raw, MASKED_SCORE)
            weight_ref[:, keys] = raw
            return jnp.maximum(highest, jnp.maximum(raw[:, :128], raw[:, 128:]))

        highest = lax.fori_loop(0, every // chunk, scores, jnp.full((count, 128), MASKED_SCORE, F32))
        highest = jnp.max(highest, axis=1, keepdims=True)

        def weights(j, total):
            keys = pl.ds(pl.multiple_of(j * chunk, chunk), chunk)
            weight = jnp.exp(weight_ref[:, keys] - highest)
            weight_ref[:, keys] = weight
            return total + (weight[:, :128] + weight[:, 128:])

        total = lax.fori_loop(0, every // chunk, weights, jnp.zeros((count, 128), F32))
        inverse = 1.0 / jnp.sum(total, axis=1, keepdims=True)
        inverse_ref[...] = inverse

        def rounded(j, nothing):
            keys = pl.ds(pl.multiple_of(j * chunk, chunk), chunk)
            probs_ref[:, keys] = (weight_ref[:, keys] * inverse).astype(BF16)
            return nothing

        lax.fori_loop(0, every // chunk, rounded, 0)

    attended = dot(probs_ref[...], v_ref[...], ((1,), (0,)))
    attended_ref[...] = attended
    reset = reset_ref[...]
    gated_ref[...] = (reset * logistic(reset) * attended).astype(BF16)


def attend(scale, at, doc, every_at, every_doc, queries, keys, values, reset_pre):
    count, zdim = queries.shape
    every, wide = values.shape
    chunk = 256
    columns = pl.BlockSpec((count, chunk), lambda c: (0, c))
    return pl.pallas_call(
        functools.partial(attend_kernel, scale),
        grid=(wide // chunk,),
        out_shape=(
            pltpu.HBM((count, every), F32),
            pltpu.HBM((count, every), BF16),
            jax.ShapeDtypeStruct((count, 1), F32),
            jax.ShapeDtypeStruct((count, wide), F32),
            jax.ShapeDtypeStruct((count, wide), BF16),
        ),
        in_specs=[
            whole(count, 1), whole(count, 1), whole(1, every), whole(1, every),
            whole(count, zdim), whole(every, zdim), pl.BlockSpec((every, chunk), lambda c: (0, c)), columns,
        ],
        out_specs=(whole(count, every), whole(count, every), whole(count, 1), columns, columns),
        compiler_params=pltpu.CompilerParams(vmem_limit_bytes=(6 + every * 7 // 2048) * MIB),
        cost_estimate=BRIEF,
        name="attend",
    )(at, doc, every_at, every_doc, queries, keys, values, reset_pre)


def middle_kernel(
    gated_ref, attended_ref, reset_ref, update_ref, cand_ref, x_ref, cot_ref, out_w_ref, up_w_ref, down_w_ref, gain_ref,
    output_ref, in_ref, hidden_ref, d_up_ref, d_tail_ref, skip_ref, gain_grad_ref, d_attended_ref, delta_ref,
    after_ref, sum_ref, normed_ref, back_ref,
):
    count, width = x_ref.shape
    wide = gated_ref.shape[1]
    chunk = 256
    for c in range(0, width, chunk):
        cols = slice(c, c + chunk)
        cand = cand_ref[:, cols] + dot(gated_ref[...], out_w_ref[:, cols], ((1,), (0,)))
        sum_ref[:, cols] = cand
        x = x_ref[:, cols].astype(F32)
        after_ref[:, cols] = x + logistic(update_ref[:, cols]) * (cand * logistic(cand) - x)
    gain = gain_ref[...]
    tall = 64
    for r in range(0, count, tall):
        rows = slice(r, r + tall)
        normed = norm_parts(after_ref[rows, :])[0]
        normed_ref[rows, :] = normed
        in_ref[rows, :] = (normed * gain).astype(BF16)
    for c in range(0, wide, chunk):
        cols = slice(c, c + chunk)
        up = dot(in_ref[...], up_w_ref[:, cols], ((1,), (0,)))
        gate = logistic(up)
        high = up * gate
        hidden_ref[:, cols] = high.astype(BF16)
        d_hidden = dot(cot_ref[...], down_w_ref[cols, :], ((1,), (1,)))
        d_up_ref[:, cols] = (d_hidden * (gate + high * (1.0 - gate))).astype(BF16)
    for c in range(0, width, chunk):
        cols = slice(c, c + chunk)
        result = after_ref[:, cols] + dot(hidden_ref[...], down_w_ref[:, cols], ((1,), (0,)))
        output_ref[:, cols] = result.astype(BF16)
        back_ref[:, cols] = dot(d_up_ref[...], up_w_ref[cols, :], ((1,), (1,)))
    gain_grad = jnp.zeros((1, width), F32)
    for r in range(0, count, tall):
        rows = slice(r, r + tall)
        back, normed, old = back_ref[rows, :], normed_ref[rows, :], after_ref[rows, :]
        inverse = norm_parts(old)[1]
        gain_grad = gain_grad + jnp.sum(back * normed, axis=0, keepdims=True)
        scaled = back * gain
        first = jnp.mean(scaled, axis=-1, keepdims=True)
        second = jnp.mean(scaled * normed, axis=-1, keepdims=True)
        d_after = cot_ref[rows, :].astype(F32) + inverse * (scaled - first - normed * second)
        update = logistic(update_ref[rows, :])
        cand = sum_ref[rows, :]
        gate = logistic(cand)
        high = cand * gate
        skip_ref[rows, :] = d_after * (1.0 - update)
        taken = d_after * update
        d_update = taken * (1.0 - update) * (high - x_ref[rows, :].astype(F32))
        d_tail_ref[rows, wide : wide + width] = d_update.astype(BF16)
        d_tail_ref[rows, wide + width :] = (taken * (gate + high * (1.0 - gate))).astype(BF16)
    gain_grad_ref[...] = gain_grad
    delta = jnp.zeros((count, 1), F32)
    for c in range(0, wide, chunk):
        cols = slice(c, c + chunk)
        d_gated = dot(d_tail_ref[:, wide + width :], out_w_ref[cols, :], ((1,), (1,)))
        attended = attended_ref[:, cols]
        reset = reset_ref[:, cols]
        gate = logistic(reset)
        high = reset * gate
        d_tail_ref[:, cols] = (d_gated * attended * (gate + high * (1.0 - gate))).astype(BF16)
        d_attended = (d_gated * high).astype(BF16)
        d_attended_ref[:, cols] = d_attended
        delta = delta + jnp.sum(d_attended.astype(F32) * attended, axis=1, keepdims=True)
    delta_ref[...] = delta


def middle(gated, attended, reset_pre, update_pre, cand_part, x, cot, w_out, w_up, w_down, gain):
    count, width = x.shape
    wide = gated.shape[1]

    def low(*shape):
        return jax.ShapeDtypeStruct(shape, BF16)

    def full(*shape):
        return jax.ShapeDtypeStruct(shape, F32)

    return pl.pallas_call(
        middle_kernel,
        out_shape=(
            low(count, width), low(count, width), low(count, wide), low(count, wide), low(count, wide + 2 * width),
            full(count, width), full(1, width), low(count, wide), full(count, 1),
        ),
        in_specs=[VMEM()] * 11,
        out_specs=(VMEM(),) * 9,
        scratch_shapes=[pltpu.VMEM((count, width), F32)] * 4,
        compiler_params=pltpu.CompilerParams(vmem_limit_bytes=28 * MIB),
        cost_estimate=BRIEF,
        name="middle",
    )(gated, attended, reset_pre, update_pre, cand_part, x, cot, w_out, w_up, w_down, gain)


def scores_back_kernel(scale, weight_ref, inverse_ref, delta_ref, d_ref, v_ref, q_ref, k_ref, near_ref, far_ref, dq_ref):
    step, steps = pl.program_id(0), pl.num_programs(0)
    d_probs = dot(d_ref[...], v_ref[...], ((1,), (1,)))
    probs = weight_ref[...] * inverse_ref[...]
    d_score = (probs * (d_probs - delta_ref[...]) * scale).astype(BF16)
    d_keys = dot(d_score, q_ref[...], ((0,), (0,))).astype(BF16)

    @pl.when(step < steps // 2)
    def _():
        near_ref[...] = d_keys

    @pl.when(step >= steps // 2)
    def _():
        far_ref[...] = d_keys

    d_queries = dot(d_score, k_ref[...], ((1,), (0,)))

    @pl.when(step == 0)
    def _():
        dq_ref[...] = d_queries

    @pl.when(step > 0)
    def _():
        dq_ref[...] += d_queries


def scores_back(scale, weight, inverse, delta, d_attended, values, queries, keys):
    count, every = weight.shape
    zdim, wide = queries.shape[1], values.shape[1]
    rows = 256
    half = every // rows // 2
    return pl.pallas_call(
        functools.partial(scores_back_kernel, scale),
        grid=(every // rows,),
        out_shape=(
            jax.ShapeDtypeStruct((every // 2, zdim), BF16),
            jax.ShapeDtypeStruct((every // 2, zdim), BF16),
            jax.ShapeDtypeStruct((count, zdim), F32),
        ),
        in_specs=[
            pl.BlockSpec((count, rows), lambda b: (0, b)), whole(count, 1), whole(count, 1), whole(count, wide),
            pl.BlockSpec((rows, wide), lambda b: (b, 0)), whole(count, zdim), pl.BlockSpec((rows, zdim), lambda b: (b, 0)),
        ],
        out_specs=(
            pl.BlockSpec((rows, zdim), lambda b: (jnp.minimum(b, half - 1), 0)),
            pl.BlockSpec((rows, zdim), lambda b: (jnp.maximum(b - half, 0), 0)),
            whole(count, zdim),
        ),
        compiler_params=pltpu.CompilerParams(vmem_limit_bytes=10 * MIB),
        cost_estimate=BRIEF,
        name="scores_back",
    )(in_hbm(weight), inverse, delta, d_attended, in_hbm(values), queries, keys)


def third_kernel(
    next_ref, dq_ref, z_ref, query_ref, key_ref, d_tail_ref, w_ref, mixed_ref, smoothed_ref, normed_ref, decay_ref,
    eta_ref, *refs
):
    *part_refs, dz_ref, zw_ref, d_ref, head_ref, omega_ref, small_ref = refs
    segs, length, width = d_ref.shape
    zdim = dq_ref.shape[1]
    d_keys = sum(part_ref[...].astype(F32) for part_ref in part_refs)
    z, d_queries = z_ref[...], dq_ref[...]
    gate = logistic(z)
    shared = z * gate
    small_ref[0:1, :] = jnp.sum(d_queries * shared, axis=0, keepdims=True)
    small_ref[1:2, :] = jnp.sum(d_queries, axis=0, keepdims=True)
    small_ref[2:3, :] = jnp.sum(d_keys * shared, axis=0, keepdims=True)
    d_shared = d_queries * query_ref[...] + d_keys * key_ref[...]
    dz_ref[...] = (d_shared * (gate + shared * (1.0 - gate))).astype(BF16)
    zw_ref[...] = dot(dz_ref[...], mixed_ref[...], ((0,), (0,))).astype(BF16)
    part = 256
    for c in range(0, width, part):
        cols = slice(c, c + part)
        back = dot(dz_ref[...], w_ref[cols, :zdim], ((1,), (1,))) + dot(d_tail_ref[...], w_ref[cols, zdim:], ((1,), (1,)))
        omega = jnp.zeros((1, part), F32)
        for i in range(segs):
            smoothed = smoothed_ref[i, :, cols]
            gate = logistic(smoothed)
            slope = gate * (1.0 + smoothed * (1.0 - gate))
            d_smoothed = back[i * length : (i + 1) * length] * slope
            d_ref[i, :, cols] = d_smoothed
            omega = omega + jnp.sum(d_smoothed * normed_ref[i, :, cols], axis=0, keepdims=True)
        omega_ref[:, cols] = omega
    part = width // 2
    for c in range(0, width, part):
        cols = slice(c, c + part)
        decay, eta = decay_ref[:, cols], eta_ref[:, cols]

        def eight(block, grads):
            at = pl.multiple_of(length - 8 - block * 8, 8)
            rows = [d_ref[i, pl.ds(at, 8), cols] for i in range(segs)]
            for u in reversed(range(8)):
                grads = tuple(
                    grad * (decay * next_ref[i, at + u]) + eta * rows[i][u : u + 1]
                    for i, grad in enumerate(grads)
                )
            return grads

        zero = jnp.zeros(decay.shape, F32)
        grads = lax.fori_loop(0, length // 8, eight, (zero,) * segs)
        for i in range(segs):
            head_ref[i, :, cols] = grads[i]


def ema_third(
    keep_next, d_queries, z_pre, query_gain, key_gain, d_tail, w_mix, mixed_in, smoothed, normed, decay, eta, *parts
):
    segs, length, width = normed.shape
    count, zdim = z_pre.shape
    return pl.pallas_call(
        third_kernel,
        out_shape=(
            jax.ShapeDtypeStruct((count, zdim), BF16),
            jax.ShapeDtypeStruct((zdim, width), BF16),
            jax.ShapeDtypeStruct(normed.shape, F32),
            jax.ShapeDtypeStruct((segs, *decay.shape), F32),
            jax.ShapeDtypeStruct((1, width), F32),
            jax.ShapeDtypeStruct((3, zdim), F32),
        ),
        in_specs=[SMEM()] + [VMEM()] * (11 + len(parts)),
        out_specs=(VMEM(),) * 6,
        compiler_params=pltpu.CompilerParams(vmem_limit_bytes=20 * MIB),
        cost_estimate=BRIEF,
        name="ema_third",
    )(keep_next, d_queries, z_pre, query_gain, key_gain, d_tail, w_mix, mixed_in, smoothed, normed, decay, eta, *parts)


def half_kernel(halved, half_ref, slot_ref, *refs):
    *refs, low_ref, high_ref = refs
    half = low_ref.shape[0]
    blocks = 2 * half
    at = 0
    for i, kind in enumerate(halved):
        left_ref, right_ref = refs[2 * i], refs[2 * i + 1]
        (count, tall), wide = left_ref.shape, right_ref.shape[1]
        piece = min(count, 2048)
        own_left = slice(None)
        if kind == "left":
            tall //= 2
            own_left = pl.ds(pl.multiple_of(half_ref[0] * tall, 128), tall)
        else:
            wide //= 2
        rows = tall // blocks
        chunk = 384
        for c in range(0, wide, chunk):
            own_right = slice(c, c + chunk)
            if kind == "right":
                own_right = pl.ds(pl.multiple_of(half_ref[0] * wide + c, 128), chunk)
            part = sum(
                dot(left_ref[k : k + piece, own_left], right_ref[k : k + piece, own_right], ((0,), (0,)))
                for k in range(0, count, piece)
            )
            for b in range(blocks):
                slot = slot_ref[b]
                own = part[b * rows : (b + 1) * rows].astype(BF16)

                @pl.when(slot < half)
                def _():
                    low_ref[slot, at : at + rows, c : c + chunk] = own

                @pl.when(slot >= half)
                def _():
                    high_ref[slot - half, at : at + rows, c : c + chunk] = own

        at += rows


def grad_half(half, slots, halved, *pairs):
    blocks = slots.shape[0]
    rows, held = 0, 0
    for i, kind in enumerate(halved):
        left, right = pairs[2 * i], pairs[2 * i + 1]
        rows += left.shape[1] // (2 if kind == "left" else 1) // blocks
        held += 2 * (left.size + right.size) + left.shape[1] * right.shape[1]
        wide = right.shape[1] // (1 if kind == "left" else 2)
    return pl.pallas_call(
        functools.partial(half_kernel, halved),
        out_shape=(jax.ShapeDtypeStruct((blocks // 2, rows, wide), BF16),) * 2,
        in_specs=[SMEM()] * 2 + [VMEM()] * len(pairs),
        out_specs=(VMEM(),) * 2,
        compiler_params=pltpu.CompilerParams(vmem_limit_bytes=held + 8 * MIB),
        cost_estimate=BRIEF,
        name="grad_half",
    )(half, slots, *pairs)


def place_kernel(halved, lead, core_ref, place_ref, own_ref, other_ref, *refs):
    wide = own_ref.shape[2]
    core = core_ref[0]
    own, other = own_ref[0].astype(F32), other_ref[0].astype(F32)
    at = 0
    for kind, out_ref in zip(halved, refs[-len(halved) :], strict=True):
        if kind == "right":
            rows = out_ref.shape[1]
            mine = pl.ds(pl.multiple_of(core * wide, 128), wide)
            others = pl.ds(pl.multiple_of((1 - core) * wide, 128), wide)
            out_ref[0, :, mine] = own[at : at + rows]
            out_ref[0, :, others] = other[at : at + rows]
        else:
            rows = out_ref.shape[2]
            if lead:
                out_ref[:, 0, :, :lead] = jnp.zeros((2, rows, lead), F32)
            out_ref[core, 0, :, lead:] = own[at : at + rows]
            out_ref[1 - core, 0, :, lead:] = other[at : at + rows]
        at += rows


def put_in_place(core, places, halved, talls, lead, own, other, before=()):
    half, rows, wide = own.shape
    blocks = 2 * half
    shapes, specs = [], []
    for kind, tall in zip(halved, talls, strict=True):
        if kind == "right":
            each = tall // blocks
            shapes.append(jax.ShapeDtypeStruct((blocks, each, 2 * wide), F32))
            specs.append(pl.BlockSpec((1, each, 2 * wide), lambda i, core, places: (places[i], 0, 0)))
        else:
            each = tall // 2 // blocks
            shapes.append(jax.ShapeDtypeStruct((2, blocks, each, lead + wide), F32))
            specs.append(pl.BlockSpec((2, 1, each, lead + wide), lambda i, core, places: (0, places[i], 0, 0)))
    block = pl.BlockSpec((1, rows, wide), lambda i, core, places: (i, 0, 0))
    return pl.pallas_call(
        functools.partial(place_kernel, halved, lead),
        out_shape=shapes,
        grid_spec=pltpu.PrefetchScalarGridSpec(
            num_scalar_prefetch=2,
            grid=(half,),
            in_specs=[block, block] + [pl.BlockSpec(memory_space=pl.ANY)] * len(before),
            out_specs=specs,
        ),
        input_output_aliases={4 + i: i for i in range(len(before))},
        compiler_params=pltpu.CompilerParams(vmem_limit_bytes=20 * MIB),
        cost_estimate=BRIEF,
        name="put_in_place",
    )(core, places, own, other, *before)


def after(value, *others):
    return lax.optimization_barrier((value, *others))[0]


def added(one, two):
    return (one.astype(F32) + two.astype(F32)).astype(one.dtype)


CORES = [(0, 1), (1, 0)]


def swapped(part):
    return lax.ppermute(part, "core", CORES)


def across(part, bit):
    chips = lax.axis_size("g") * lax.axis_size("s")
    return lax.ppermute(part, ("g", "s"), [(i, i ^ (1 << bit)) for i in range(chips)])


class Lane:
    def __init__(self, order, back, halved):
        chips = lax.axis_size("g") * lax.axis_size("s")
        bits = chips.bit_length() - 1
        order = list(order) + [bit for bit in range(bits) if bit not in order]
        self.cut, self.rest, self.halved = order[:3], order[3:], halved
        chip = lax.axis_index(("g", "s"))
        self.core = lax.axis_index("core").reshape(1)
        block = jnp.arange(1 << len(self.cut), dtype=jnp.int32)
        count = len(self.cut)
        self.slots = block ^ sum(((chip >> bit) & 1) << (count - 1 - t) for t, bit in enumerate(self.cut))
        self.back = [bit for bit in back if bit in self.cut]
        self.back_slots = sum(
            (((block >> (count - 1 - t)) ^ (chip >> bit)) & 1) << self.back.index(bit) for t, bit in enumerate(self.cut)
        )

    def theirs(self, *pairs):
        self.talls = [left.shape[1] for left in pairs[::2]]
        low, high = grad_half(1 - self.core, self.slots, self.halved, *pairs)
        self.received, self.received_low = swapped(high), swapped(low)
        return high

    def mine(self, *pairs):
        self.low, self.kept = grad_half(self.core, self.slots, self.halved, *pairs)
        self.turn = 0
        return self.kept

    def more(self):
        return self.turn < 2 * len(self.cut) + len(self.rest)

    def near_end(self):
        return self.turn >= 2 * len(self.cut) + len(self.rest) - 1

    def step(self, *others):
        received = after(self.received, *others)
        cut, rest = self.cut, self.rest
        doubled = self.turn - len(cut) - len(rest)
        if self.turn == 0:
            self.sent = added(self.kept, received)
            self.kept = added(self.low, after(self.received_low, self.sent))
            bit = cut[0]
        elif self.turn < len(cut):
            half = self.kept.shape[0] // 2
            self.sent = added(self.kept[half:], received[half:])
            self.kept = added(self.kept[:half], received[:half])
            bit = cut[self.turn]
        elif doubled < 0:
            self.sent = self.kept = added(self.kept, received)
            bit = rest[self.turn - len(cut)]
        elif doubled == 0:
            self.sent = added(self.kept, received)
            bit = self.back[0]
        else:
            self.sent = jnp.concatenate([self.sent, received])
            bit = self.back[doubled]
        self.received = across(self.sent, bit)
        self.turn += 1
        return self.sent

    def end_near(self, last, lead=0):
        self.lead = lead
        other = after(swapped(self.sent), last)
        half = self.sent.shape[0]
        slot = jnp.arange(2 * half, dtype=jnp.int32)
        self.places = jnp.sum(jnp.where(self.back_slots[None] == slot[:, None], slot[None], 0), axis=1, dtype=jnp.int32)
        self.outs = put_in_place(self.core, self.places[:half], self.halved, self.talls, lead, self.sent, other)
        return self.outs[0]

    def arrive(self, *others):
        self.received = after(self.received, *others)
        self.other = swapped(self.received)
        return self.received

    def end(self, last):
        half = self.sent.shape[0]
        outs = put_in_place(
            self.core, self.places[half:], self.halved, self.talls, self.lead,
            self.received, after(self.other, last), self.outs,
        )
        return [out.reshape(tall, -1) for out, tall in zip(outs, self.talls, strict=True)]


def local(
    tokens,
    cotangent,
    doc_lengths,
    attn_gain,
    ema_beta,
    alpha_raw,
    delta_raw,
    ema_eta,
    ema_omega,
    w_value,
    w_mix,
    query_gain,
    query_bias,
    key_gain,
    w_out,
    ffn_gain,
    w_up,
    w_down,
):
    held, seg_len, width = tokens.shape
    planes, around = lax.axis_size("g"), lax.axis_size("s")
    g, s, core = lax.axis_index("g"), lax.axis_index("s"), lax.axis_index("core")
    odd = g % 2
    count = 2 * seg_len
    zdim = query_gain.shape[0]
    vdim = w_value.shape[1]
    scale_factor = zdim ** (-0.5)

    def number(z, x, c):
        return (z * around + x) * 2 + c

    routes = [
        [
            (number(z, x, c), number(2 * c + ((z % 2) ^ a), x, z // 2))
            for z in range(planes)
            for x in range(around)
            for c in range(2)
        ]
        for a in range(2)
    ]

    def to_planes(rows):
        return jnp.concatenate(
            [
                lax.ppermute(lax.dynamic_slice_in_dim(rows, odd ^ a, 1, 0), EVERY, routes[a])
                for a in range(2)
            ]
        )

    def from_planes(segs):
        return [
            lax.ppermute(segs[a : a + 1], EVERY, [(b, a_) for a_, b in routes[a]])
            for a in range(2)
        ]

    def in_order(back):
        return jnp.concatenate(
            [jnp.where(odd == 0, back[0], back[1]), jnp.where(odd == 0, back[1], back[0])]
        )

    def nearby(part, k):
        return lax.ppermute(part, "s", [(i, i ^ k) for i in range(around)])

    def gathered_near(part):
        return jnp.concatenate([part] + [nearby(part, k) for k in range(1, around)])

    def gathered(part):
        near = gathered_near(part)
        return jnp.concatenate([near, swapped(near)])

    hops = range(around.bit_length() - 1)

    def hop_gather(part, hop):
        return jnp.concatenate([part, nearby(part, 1 << hop)])

    def hop_send(parts, hop):
        half = parts.shape[0] // 2
        return parts[:half], nearby(parts[half:], 1 << hop)

    def scattered_near(parts, received):
        mine = added(parts, received).reshape(around, parts.shape[0] // around, *parts.shape[1:])
        return mine, [nearby(mine[k], k) for k in range(1, around)]

    def scattered_sum(mine, received):
        total = mine[0].astype(F32)
        for part in received:
            total = total + part.astype(F32)
        return total

    x_rows = to_planes(tokens)

    other = lax.ppermute(doc_lengths, "core", [(0, 1), (1, 0)])
    lengths = jnp.where(g // 2 == core, doc_lengths[odd], other[odd])
    docs = lengths.shape[0]
    before_it = jnp.arange(docs)[:, None] > jnp.arange(docs)[None, :]
    starts = jnp.sum(jnp.where(before_it, lengths[None, :], 0), axis=1)

    def doc_of(positions):
        return jnp.sum((starts[:, None] <= positions[None, :]).astype(jnp.int32), axis=0) - 1

    def kept_at(positions):
        return 1.0 - jnp.any(starts[:, None] == positions[None, :], axis=0).astype(F32)

    def blocks_of(s_of, core_of):
        return [(2 * core_of + (odd ^ i)) * around + s_of for i in range(2)]

    place = jnp.stack(blocks_of(s, core))
    order = jnp.stack(
        [block for c in range(2) for k in range(around) for block in blocks_of(s ^ k, core ^ c)]
    )
    n_segs = order.shape[0]
    block = jnp.arange(n_segs, dtype=jnp.int32)
    other_core = (block // around // 2) ^ core
    near_slots = (other_core * around + ((block % around) ^ s)) * 2 + ((block // around % 2) ^ odd)
    within = jnp.arange(seg_len, dtype=jnp.int32)
    local_pos = (place[:, None] * seg_len + within).reshape(-1)
    every_pos = (order[:, None] * seg_len + within).reshape(-1)
    keep = kept_at(local_pos).reshape(2, seg_len)
    keep_next = kept_at(local_pos + 1).reshape(2, seg_len)
    row_keep = kept_at(jnp.arange(n_segs * seg_len + 1, dtype=jnp.int32))
    passes = jnp.min(row_keep[:-1].reshape(n_segs, seg_len), axis=1)
    passes_back = jnp.min(row_keep[1:].reshape(n_segs, seg_len), axis=1)

    ema_alpha = jax.nn.sigmoid(alpha_raw)
    ema_delta = jax.nn.sigmoid(delta_raw)
    decay = 1.0 - ema_alpha * ema_delta
    feed_gain = ema_alpha * ema_beta
    long_decay = decay
    reach = 1
    while reach < seg_len:
        long_decay = long_decay * long_decay
        reach *= 2
    gain_row, omega_row = attn_gain[None], ema_omega[None]

    normed_rows, ends = ema_first(keep, x_rows, gain_row, decay, feed_gain)
    near_ends = gathered_near(ends)
    every_end = jnp.concatenate([near_ends, swapped(near_ends)])
    every_x = gathered(after(x_rows, near_ends))
    cot_rows = to_planes(after(cotangent, near_ends))
    smoothed, mixed_in, states_enter = ema_second(
        place, near_slots, passes, keep, normed_rows, every_end, long_decay, decay, feed_gain, ema_eta, omega_row
    )
    mixed_in = mixed_in.reshape(count, width)

    z_pre = dot(mixed_in, w_mix[:, :zdim], ((1,), (0,)))
    shared = jax.nn.silu(z_pre)
    queries = (shared * query_gain + query_bias).astype(BF16)
    keys = (shared * key_gain).astype(BF16)
    every_key = gathered(keys)
    every_normed, values, value_slope = row_values(after(every_x, keys), gain_row, w_value)
    mixed_here = after(mixed_in, keys)
    reset_pre = dot(mixed_here, w_mix[:, zdim : zdim + vdim], ((1,), (0,)))
    update_pre = dot(mixed_here, w_mix[:, zdim + vdim : zdim + vdim + width], ((1,), (0,)))
    cand_part = dot(mixed_here, w_mix[:, zdim + vdim + width :], ((1,), (0,)))

    inputs_x = x_rows.reshape(count, width)
    weight, probs_low, inverse, attended, gated = attend(
        scale_factor, local_pos[:, None], doc_of(local_pos)[:, None], every_pos[None], doc_of(every_pos)[None],
        queries, every_key, values, reset_pre,
    )
    cot_flat = cot_rows.reshape(count, width)
    result, ffn_in, hidden, d_up, d_tail, d_skip, grad_ffn_gain, d_attended, delta_row = middle(
        gated, attended, reset_pre, update_pre, cand_part, inputs_x, cot_flat, w_out, w_up, w_down, ffn_gain[None]
    )
    d_cand = d_tail[:, vdim + width :]

    one, two = Lane((2, 0, 1, 3), (2, 1, 0), ("left", "right")), Lane((1, 0, 2, 3), (0, 1, 2), ("right",))
    three, four = Lane((2, 1, 0, 3), (0, 2, 1), ("left",)), Lane((0, 1, 2, 3), (0, 1, 2), ("left",))

    def all_step(last, *lanes):
        for lane in lanes:
            if lane.more():
                last = lane.step(last)
        return last

    last = one.theirs(gated, d_cand, ffn_in, d_up)
    last = three.theirs(after(mixed_in, last), d_tail)
    keys_sums, keys_far, d_queries = scores_back(
        scale_factor, weight, inverse, after(delta_row, last), d_attended, values, queries, every_key
    )
    keys_swapped = swapped(keys_far)
    last = one.mine(gated, d_cand, after(ffn_in, d_queries), d_up)
    last = one.step(last)
    keys_sums = added(keys_sums, after(keys_swapped, last))
    last = keys_sums
    for hop in reversed(hops):
        keys_kept, keys_near = hop_send(keys_sums, hop)
        if hop == hops[-1]:
            last = three.mine(after(mixed_in, last), d_tail)
            last = three.step(last)
            last = four.theirs(hidden, after(cot_flat, last))
        if hop > 0:
            keys_sums = added(keys_kept, after(keys_near, last))
            last = keys_sums
    last = four.mine(hidden, after(cot_flat, last))
    last = four.step(last)
    d_value_pre, normed_near_part, normed_far = values_back(
        after(probs_low, last), d_attended, value_slope, w_value
    )
    d_z_pre, grad_z, d_smoothed, grad_heads, grad_omega, grad_z_small = ema_third(
        keep_next, d_queries, z_pre, query_gain[None], key_gain[None], d_tail, w_mix, mixed_in, smoothed, normed_rows,
        decay, ema_eta, keys_kept, after(keys_near, d_value_pre),
    )
    heads = grad_heads
    for hop in hops:
        near = nearby(heads, 1 << hop)
        if hop == 0:
            last = two.theirs(every_normed, after(d_value_pre, heads))
            last = four.step(last)
            near = after(near, last)
        if hop == hops[-1]:
            last = two.mine(every_normed, after(d_value_pre, heads))
            near = after(near, last)
        heads = jnp.concatenate([heads, near])
    far = swapped(heads)
    normed_swapped = swapped(after(normed_far, heads))
    last = one.step(heads)
    last = two.step(last)
    every_head = jnp.concatenate([heads, after(far, last)])
    normed_sums = added(normed_near_part, after(normed_swapped, every_head))
    ema_normed, grad_rates = ema_fourth(
        place, near_slots, passes_back, keep, keep_next, d_smoothed, normed_rows, states_enter, every_head,
        long_decay, decay, feed_gain, ema_eta, omega_row, ema_alpha, ema_delta, ema_beta, grad_omega,
    )
    output = from_planes(after(result, grad_rates).reshape(2, seg_len, width))
    last = all_step(grad_rates, three, four, two, one)
    normed_kept, normed_near = hop_send(after(normed_sums, last, *output), hops[-1])
    output = in_order(output)
    last = all_step(last, three, four, two, one)
    for hop in reversed(hops[:-1]):
        last = added(normed_kept, after(normed_near, last))
        normed_kept, normed_near = hop_send(last, hop)
    last = all_step(last, three, four, two, one)
    d_normed = normed_kept.astype(F32) + after(normed_near, last).astype(F32)
    normed_one, inverse_one = norm_parts(inputs_x.astype(F32))
    d_norm_one, grad_attn_gain = norm_back(
        d_normed + ema_normed.reshape(count, width), normed_one, inverse_one, attn_gain
    )
    back = (d_skip + d_norm_one).astype(BF16)
    gains = jnp.concatenate(
        [
            grad_attn_gain[None],
            grad_omega,
            grad_ffn_gain,
            jnp.pad(grad_z_small.reshape(1, -1), ((0, 0), (0, width - 3 * zdim))),
            jnp.zeros((12, width), F32),
        ]
    )
    small = jnp.concatenate([grad_rates, gains.astype(BF16), grad_z])
    tall = small.shape[0] // 2
    small_far = lax.dynamic_slice_in_dim(small, (1 - core) * tall, tall)
    small_own = lax.dynamic_slice_in_dim(small, core * tall, tall)
    small, last = small_own, (small_far,)
    for bit in [None] + list(range((planes * around).bit_length() - 1)):
        small_near = swapped(small_far) if bit is None else across(after(small, *last), bit)
        last = all_step(small, *(lane for lane in (one, three, four, two) if not lane.near_end()))
        small = added(small, after(small_near, last))
        last = (small,)
        if bit == 0:
            sent_back = from_planes(after(back, small).reshape(2, seg_len, width))
        if bit == 1:
            last = (small, *sent_back)
    grad_tokens = in_order(sent_back).astype(F32)
    small_near = swapped(after(small, *last))
    last = small
    while not all(lane.near_end() for lane in (one, two, three, four)):
        last = all_step(last, *(lane for lane in (one, three, four, two) if not lane.near_end()))
    order_of_end = four, one, two, three
    last = all_step(last, *order_of_end)
    ended = {}
    for lane in order_of_end:
        last = lane.end_near(last, zdim if lane is three else 0)
    for lane in order_of_end:
        last = lane.arrive(last)
    for lane in order_of_end:
        ended[lane] = lane.end(last)
        last = ended[lane][0]
    small_near = after(small_near, last)
    small = jnp.where(core == 0, jnp.concatenate([small, small_near]), jnp.concatenate([small_near, small]))
    small = small.astype(F32)
    (grad_wout, grad_up), (grad_value,), (grad_mix,), (grad_down,) = (ended[lane] for lane in (one, two, three, four))
    grad_mix = lax.dynamic_update_slice(grad_mix, small[-zdim:].T, (0, 0))
    n_heads = decay.shape[0]
    grad_beta, grad_alpha, grad_delta, grad_eta = (small[i * n_heads : (i + 1) * n_heads] for i in range(4))
    grad_attn_gain, grad_omega, grad_ffn_gain, last = (small[4 * n_heads + i] for i in range(4))
    grad_qgain, grad_qbias, grad_kgain = (last[i * zdim : (i + 1) * zdim] for i in range(3))
    return (
        output,
        grad_tokens,
        grad_attn_gain,
        grad_beta,
        grad_alpha,
        grad_delta,
        grad_eta,
        grad_omega,
        grad_value,
        grad_mix,
        grad_qgain,
        grad_qbias,
        grad_kgain,
        grad_wout,
        grad_ffn_gain,
        grad_up,
        grad_down,
    )


def solution(mesh):
    devices = mesh.devices
    finer = Mesh(devices.reshape(4, devices.shape[0] // 4, 2), EVERY)
    split = P("core", ("g", "s"), None)
    placed = (split, split, P("core", None)) + (P(),) * 15
    return jax.shard_map(
        local,
        mesh=finer,
        in_specs=placed,
        out_specs=(split, split) + (P(),) * 15,
        check_vma=False,
    )
```

```python
import functools

import jax
import jax.numpy as jnp
from jax import lax
from jax.experimental import pallas as pl
from jax.experimental.pallas import tpu as pltpu
from jax.sharding import Mesh
from jax.sharding import PartitionSpec as P

EPSILON = 1e-05
MASKED_SCORE = -1e30
BF16 = jnp.bfloat16
F32 = jnp.float32
EVERY = ("g", "s", "core")
MIB = 1024 * 1024
BRIEF = pl.CostEstimate(flops=1, bytes_accessed=1, transcendentals=0)


def logistic(inputs):
    return 0.5 * jnp.tanh(0.5 * inputs) + 0.5


def silu_slope(inputs):
    gate = logistic(inputs)
    return gate * (1.0 + inputs * (1.0 - gate))


def norm_parts(inputs):
    centred = inputs - jnp.mean(inputs, axis=-1, keepdims=True)
    inverse = lax.rsqrt(jnp.mean(centred * centred, axis=-1, keepdims=True) + EPSILON)
    return (centred * inverse, inverse)


def norm_back(upstream, normed, inverse, gain):
    scaled = upstream * gain
    first_mean = jnp.mean(scaled, axis=-1, keepdims=True)
    second_mean = jnp.mean(scaled * normed, axis=-1, keepdims=True)
    return (
        inverse * (scaled - first_mean - normed * second_mean),
        jnp.sum(upstream * normed, axis=0),
    )


def dot(left, right, contract):
    return lax.dot_general(left, right, (contract, ((), ())), preferred_element_type=F32)


SMEM = functools.partial(pl.BlockSpec, memory_space=pltpu.SMEM)


def in_hbm(value):
    return pltpu.with_memory_space_constraint(value, pltpu.HBM)


def whole(*shape):
    return pl.BlockSpec(shape, lambda *_: (0,) * len(shape))


def first_kernel(keep_ref, x_ref, gain_ref, decay_ref, feed_ref, normed_ref, last_ref):
    segs, length, width = x_ref.shape
    for i in range(segs):
        normed_ref[i] = norm_parts(x_ref[i].astype(F32))[0] * gain_ref[...]
    part = width // 2
    for c in range(0, width, part):
        cols = slice(c, c + part)
        decay, feed = decay_ref[:, cols], feed_ref[:, cols]

        def eight(block, states):
            at = pl.multiple_of(block * 8, 8)
            rows = [normed_ref[i, pl.ds(at, 8), cols] for i in range(segs)]
            for u in range(8):
                states = tuple(
                    state * (decay * keep_ref[i, at + u]) + feed * rows[i][u : u + 1]
                    for i, state in enumerate(states)
                )
            return states

        zero = jnp.zeros(decay.shape, F32)
        states = lax.fori_loop(0, length // 8, eight, (zero,) * segs)
        for i in range(segs):
            last_ref[i, :, cols] = states[i]


def ema_first(keep, x, gain, decay, feed):
    segs, length, width = x.shape
    return pl.pallas_call(
        first_kernel,
        out_shape=(
            jax.ShapeDtypeStruct(x.shape, F32),
            jax.ShapeDtypeStruct((segs, *decay.shape), F32),
        ),
        in_specs=[SMEM()] + [pl.BlockSpec(memory_space=pltpu.VMEM)] * 4,
        out_specs=(pl.BlockSpec(memory_space=pltpu.VMEM),) * 2,
        compiler_params=pltpu.CompilerParams(vmem_limit_bytes=8 * MIB),
        cost_estimate=BRIEF,
        name="ema_first",
    )(keep, x, gain, decay, feed)


def second_kernel(
    place_ref, slot_ref, pass_ref, keep_ref, normed_ref, ends_ref, long_ref, decay_ref, feed_ref, eta_ref, omega_ref,
    smoothed_ref, mixed_ref, enter_ref,
):
    segs, length, width = normed_ref.shape
    for i in range(segs):

        def hop(p, state):
            return state * (long_ref[...] * pass_ref[p]) + ends_ref[slot_ref[p]]

        enter_ref[i] = lax.fori_loop(0, place_ref[i], hop, jnp.zeros(decay_ref.shape, F32))

    part = width // 2
    for c in range(0, width, part):
        cols = slice(c, c + part)
        decay, feed, eta = decay_ref[:, cols], feed_ref[:, cols], eta_ref[:, cols]
        omega = omega_ref[:, cols]

        def eight(block, states):
            at = pl.multiple_of(block * 8, 8)
            rows = [normed_ref[i, pl.ds(at, 8), cols] for i in range(segs)]
            sums = [[] for _ in range(segs)]
            for u in range(8):
                following = []
                for i, state in enumerate(states):
                    state = state * (decay * keep_ref[i, at + u]) + feed * rows[i][u : u + 1]
                    sums[i].append(jnp.sum(eta * state, axis=0, keepdims=True))
                    following.append(state)
                states = tuple(following)
            for i in range(segs):
                smooth = jnp.concatenate(sums[i], axis=0) + omega * rows[i]
                smoothed_ref[i, pl.ds(at, 8), cols] = smooth
            return states

        lax.fori_loop(0, length // 8, eight, tuple(enter_ref[i, :, cols] for i in range(segs)))
    smoothed = smoothed_ref[...]
    mixed_ref[...] = (smoothed * logistic(smoothed)).astype(BF16)


VMEM = functools.partial(pl.BlockSpec, memory_space=pltpu.VMEM)


def ema_second(place, slots, passes, keep, normed, ends, long_decay, decay, feed, eta, omega):
    segs, length, width = normed.shape
    return pl.pallas_call(
        second_kernel,
        out_shape=(
            jax.ShapeDtypeStruct(normed.shape, F32),
            jax.ShapeDtypeStruct(normed.shape, BF16),
            jax.ShapeDtypeStruct((segs, *decay.shape), F32),
        ),
        in_specs=[SMEM()] * 4 + [VMEM()] * 7,
        out_specs=(VMEM(),) * 3,
        compiler_params=pltpu.CompilerParams(vmem_limit_bytes=12 * MIB),
        cost_estimate=BRIEF,
        name="ema_second",
    )(place, slots, passes, keep, normed, ends, long_decay, decay, feed, eta, omega)


def fourth_kernel(
    place_ref, slot_ref, pass_ref, keep_ref, next_ref, d_ref, normed_ref, enter_ref, heads_ref, long_ref,
    decay_ref, feed_ref, eta_ref, omega_ref, alpha_ref, delta_ref, beta_ref, omega_grad_ref, grad_ref, rates_ref, before_ref,
):
    segs, length, width = normed_ref.shape
    n_heads = decay_ref.shape[0]
    half = width // 2
    for c in range(0, width, half):
        cols = slice(c, c + half)
        decay, feed = decay_ref[:, cols], feed_ref[:, cols]

        def again(block, states):
            at = pl.multiple_of(block * 8, 8)
            rows = [normed_ref[i, pl.ds(at, 8), cols] for i in range(segs)]
            for u in range(8):
                following = []
                for i, state in enumerate(states):
                    state = state * keep_ref[i, at + u]
                    before_ref[i, at + u, :, cols] = state
                    following.append(state * decay + feed * rows[i][u : u + 1])
                states = tuple(following)
            return states

        lax.fori_loop(0, length // 8, again, tuple(enter_ref[i, :, cols] for i in range(segs)))

    count = slot_ref.shape[0]
    part = width // 3
    for c in range(0, width, part):
        cols = slice(c, c + part)
        decay, feed, eta = decay_ref[:, cols], feed_ref[:, cols], eta_ref[:, cols]
        omega = omega_ref[:, cols]
        entering = []
        for i in range(segs):

            def hop(back, grad):
                p = count - 1 - back
                return grad * (long_ref[:, cols] * pass_ref[p]) + heads_ref[slot_ref[p], :, cols]

            entering.append(lax.fori_loop(0, count - 1 - place_ref[i], hop, jnp.zeros(decay.shape, F32)))

        def eight(block, carried):
            grads, kept, decayed, fed = carried
            at = pl.multiple_of(length - 8 - block * 8, 8)
            rows = [normed_ref[i, pl.ds(at, 8), cols] for i in range(segs)]
            d_rows = [d_ref[i, pl.ds(at, 8), cols] for i in range(segs)]
            sums = [[] for _ in range(segs)]
            for u in reversed(range(8)):
                following = []
                for i, grad in enumerate(grads):
                    d_row = d_rows[i][u : u + 1]
                    grad = grad * (decay * next_ref[i, at + u]) + eta * d_row
                    before = before_ref[i, at + u, :, cols]
                    kept = kept + d_row * before
                    decayed = decayed + grad * before
                    fed = fed + grad * rows[i][u : u + 1]
                    sums[i].insert(0, jnp.sum(feed * grad, axis=0, keepdims=True))
                    following.append(grad)
                grads = tuple(following)
            for i in range(segs):
                grad_ref[i, pl.ds(at, 8), cols] = jnp.concatenate(sums[i], axis=0) + omega * d_rows[i]
            return grads, kept, decayed, fed

        zero = jnp.zeros(decay.shape, F32)
        _, kept, decayed, fed = lax.fori_loop(0, length // 8, eight, (tuple(entering), zero, zero, zero))
        alpha, delta = alpha_ref[:, cols], delta_ref[:, cols]
        made = (
            alpha * fed,
            alpha * (1.0 - alpha) * (beta_ref[:, cols] * fed - delta * decayed),
            -delta * (1.0 - delta) * alpha * decayed,
            decay * kept + feed * omega_grad_ref[:, cols],
        )
        for i, gradient in enumerate(made):
            rates_ref[i * n_heads : (i + 1) * n_heads, cols] = gradient.astype(BF16)


def ema_fourth(
    place, slots, passes, keep, keep_next, d_smoothed, normed, enter, heads_grad, long_decay, decay, feed, eta, omega,
    alpha, delta, beta, omega_grad,
):
    segs, length, width = normed.shape
    return pl.pallas_call(
        fourth_kernel,
        out_shape=(
            jax.ShapeDtypeStruct(normed.shape, F32),
            jax.ShapeDtypeStruct((4 * decay.shape[0], width), BF16),
        ),
        in_specs=[SMEM()] * 5 + [VMEM()] * 13,
        out_specs=(VMEM(),) * 2,
        scratch_shapes=[pltpu.VMEM((segs, length, *decay.shape), F32)],
        compiler_params=pltpu.CompilerParams(vmem_limit_bytes=24 * MIB),
        cost_estimate=BRIEF,
        name="ema_fourth",
    )(
        place, slots, passes, keep, keep_next, d_smoothed, normed, enter, heads_grad, long_decay, decay, feed, eta, omega,
        alpha, delta, beta, omega_grad,
    )


def values_kernel(x_ref, gain_ref, w_ref, normed_ref, values_ref, slope_ref):
    segs, length, width = x_ref.shape
    x = x_ref[...].astype(F32).reshape(segs * length, width)
    normed = (norm_parts(x)[0] * gain_ref[...]).astype(BF16)
    normed_ref[...] = normed
    wide = w_ref.shape[1]
    chunk = wide // 3
    for c in range(0, wide, chunk):
        pre = dot(normed, w_ref[:, c : c + chunk], ((1,), (0,)))
        gate = logistic(pre)
        value = pre * gate
        values_ref[:, c : c + chunk] = value.astype(BF16)
        slope_ref[:, c : c + chunk] = (gate + value * (1.0 - gate)).astype(BF16)


def row_values(x, gain, w_value):
    segs, length, width = x.shape
    wide = w_value.shape[1]
    rows = 2 * length
    count = segs * length
    return pl.pallas_call(
        values_kernel,
        grid=(segs // 2,),
        out_shape=(
            pltpu.HBM((count, width), BF16),
            jax.ShapeDtypeStruct((count, wide), BF16),
            pltpu.HBM((count, wide), BF16),
        ),
        in_specs=[pl.BlockSpec((2, length, width), lambda b: (b, 0, 0)), whole(1, width), whole(width, wide)],
        out_specs=(
            pl.BlockSpec((rows, width), lambda b: (b, 0)),
            pl.BlockSpec((rows, wide), lambda b: (b, 0)),
            pl.BlockSpec((rows, wide), lambda b: (b, 0)),
        ),
        compiler_params=pltpu.CompilerParams(vmem_limit_bytes=16 * MIB),
        cost_estimate=BRIEF,
        name="row_values",
    )(x, gain, in_hbm(w_value))


def values_back_kernel(probs_ref, d_ref, slope_ref, w_ref, pre_ref, near_ref, far_ref):
    wide = d_ref.shape[1]
    chunk = wide // 3
    total = jnp.zeros(near_ref.shape, F32)
    for c in range(0, wide, chunk):
        cols = slice(c, c + chunk)
        d_values = dot(probs_ref[...], d_ref[:, cols], ((0,), (0,)))
        pre = (d_values * slope_ref[:, cols].astype(F32)).astype(BF16)
        pre_ref[:, cols] = pre
        total = total + dot(pre, w_ref[:, cols], ((1,), (1,)))
    step, steps = pl.program_id(0), pl.num_programs(0)

    @pl.when(step < steps // 2)
    def _():
        near_ref[...] = total.astype(BF16)

    @pl.when(step >= steps // 2)
    def _():
        far_ref[...] = total.astype(BF16)


def values_back(probs, d_attended, slope, w_value):
    count, every = probs.shape
    width, wide = w_value.shape
    rows = 256
    half = every // rows // 2
    return pl.pallas_call(
        values_back_kernel,
        grid=(every // rows,),
        out_shape=(
            jax.ShapeDtypeStruct((every, wide), BF16),
            jax.ShapeDtypeStruct((every // 2, width), BF16),
            jax.ShapeDtypeStruct((every // 2, width), BF16),
        ),
        in_specs=[
            pl.BlockSpec((count, rows), lambda b: (0, b)),
            whole(count, wide),
            pl.BlockSpec((rows, wide), lambda b: (b, 0)),
            whole(width, wide),
        ],
        out_specs=(
            pl.BlockSpec((rows, wide), lambda b: (b, 0)),
            pl.BlockSpec((rows, width), lambda b: (jnp.minimum(b, half - 1), 0)),
            pl.BlockSpec((rows, width), lambda b: (jnp.maximum(b - half, 0), 0)),
        ),
        compiler_params=pltpu.CompilerParams(vmem_limit_bytes=16 * MIB),
        cost_estimate=BRIEF,
        name="values_back",
    )(in_hbm(probs), d_attended, in_hbm(slope), in_hbm(w_value))


def attend_kernel(
    scale, at_ref, doc_ref, every_at_ref, every_doc_ref, q_ref, k_ref, v_ref, reset_ref,
    weight_ref, probs_ref, inverse_ref, attended_ref, gated_ref,
):
    count, every = probs_ref.shape
    chunk = 256

    @pl.when(pl.program_id(0) == 0)
    def _():
        def scores(j, highest):
            keys = pl.ds(pl.multiple_of(j * chunk, chunk), chunk)
            raw = dot(q_ref[...], k_ref[keys, :], ((1,), (1,))) * scale
            visible = (every_doc_ref[:, keys] == doc_ref[...]) & (every_at_ref[:, keys] <= at_ref[...])
            raw = jnp.where(visible, raw, MASKED_SCORE)
            weight_ref[:, keys] = raw
            return jnp.maximum(highest, jnp.maximum(raw[:, :128], raw[:, 128:]))

        highest = lax.fori_loop(0, every // chunk, scores, jnp.full((count, 128), MASKED_SCORE, F32))
        highest = jnp.max(highest, axis=1, keepdims=True)

        def weights(j, total):
            keys = pl.ds(pl.multiple_of(j * chunk, chunk), chunk)
            weight = jnp.exp(weight_ref[:, keys] - highest)
            weight_ref[:, keys] = weight
            return total + (weight[:, :128] + weight[:, 128:])

        total = lax.fori_loop(0, every // chunk, weights, jnp.zeros((count, 128), F32))
        inverse = 1.0 / jnp.sum(total, axis=1, keepdims=True)
        inverse_ref[...] = inverse

        def rounded(j, nothing):
            keys = pl.ds(pl.multiple_of(j * chunk, chunk), chunk)
            probs_ref[:, keys] = (weight_ref[:, keys] * inverse).astype(BF16)
            return nothing

        lax.fori_loop(0, every // chunk, rounded, 0)

    attended = dot(probs_ref[...], v_ref[...], ((1,), (0,)))
    attended_ref[...] = attended
    reset = reset_ref[...]
    gated_ref[...] = (reset * logistic(reset) * attended).astype(BF16)


def attend(scale, at, doc, every_at, every_doc, queries, keys, values, reset_pre):
    count, zdim = queries.shape
    every, wide = values.shape
    chunk = 256
    columns = pl.BlockSpec((count, chunk), lambda c: (0, c))
    return pl.pallas_call(
        functools.partial(attend_kernel, scale),
        grid=(wide // chunk,),
        out_shape=(
            pltpu.HBM((count, every), F32),
            pltpu.HBM((count, every), BF16),
            jax.ShapeDtypeStruct((count, 1), F32),
            jax.ShapeDtypeStruct((count, wide), F32),
            jax.ShapeDtypeStruct((count, wide), BF16),
        ),
        in_specs=[
            whole(count, 1), whole(count, 1), whole(1, every), whole(1, every),
            whole(count, zdim), whole(every, zdim), pl.BlockSpec((every, chunk), lambda c: (0, c)), columns,
        ],
        out_specs=(whole(count, every), whole(count, every), whole(count, 1), columns, columns),
        compiler_params=pltpu.CompilerParams(vmem_limit_bytes=(6 + every * 7 // 2048) * MIB),
        cost_estimate=BRIEF,
        name="attend",
    )(at, doc, every_at, every_doc, queries, keys, values, reset_pre)


def middle_kernel(
    gated_ref, attended_ref, reset_ref, update_ref, cand_ref, x_ref, cot_ref, out_w_ref, up_w_ref, down_w_ref, gain_ref,
    output_ref, in_ref, hidden_ref, d_up_ref, d_tail_ref, skip_ref, gain_grad_ref, d_attended_ref, delta_ref,
    after_ref, sum_ref, normed_ref, back_ref,
):
    count, width = x_ref.shape
    wide = gated_ref.shape[1]
    chunk = 256
    for c in range(0, width, chunk):
        cols = slice(c, c + chunk)
        cand = cand_ref[:, cols] + dot(gated_ref[...], out_w_ref[:, cols], ((1,), (0,)))
        sum_ref[:, cols] = cand
        x = x_ref[:, cols].astype(F32)
        after_ref[:, cols] = x + logistic(update_ref[:, cols]) * (cand * logistic(cand) - x)
    gain = gain_ref[...]
    tall = 64
    for r in range(0, count, tall):
        rows = slice(r, r + tall)
        normed = norm_parts(after_ref[rows, :])[0]
        normed_ref[rows, :] = normed
        in_ref[rows, :] = (normed * gain).astype(BF16)
    for c in range(0, wide, chunk):
        cols = slice(c, c + chunk)
        up = dot(in_ref[...], up_w_ref[:, cols], ((1,), (0,)))
        gate = logistic(up)
        high = up * gate
        hidden_ref[:, cols] = high.astype(BF16)
        d_hidden = dot(cot_ref[...], down_w_ref[cols, :], ((1,), (1,)))
        d_up_ref[:, cols] = (d_hidden * (gate + high * (1.0 - gate))).astype(BF16)
    for c in range(0, width, chunk):
        cols = slice(c, c + chunk)
        result = after_ref[:, cols] + dot(hidden_ref[...], down_w_ref[:, cols], ((1,), (0,)))
        output_ref[:, cols] = result.astype(BF16)
        back_ref[:, cols] = dot(d_up_ref[...], up_w_ref[cols, :], ((1,), (1,)))
    gain_grad = jnp.zeros((1, width), F32)
    for r in range(0, count, tall):
        rows = slice(r, r + tall)
        back, normed, old = back_ref[rows, :], normed_ref[rows, :], after_ref[rows, :]
        inverse = norm_parts(old)[1]
        gain_grad = gain_grad + jnp.sum(back * normed, axis=0, keepdims=True)
        scaled = back * gain
        first = jnp.mean(scaled, axis=-1, keepdims=True)
        second = jnp.mean(scaled * normed, axis=-1, keepdims=True)
        d_after = cot_ref[rows, :].astype(F32) + inverse * (scaled - first - normed * second)
        update = logistic(update_ref[rows, :])
        cand = sum_ref[rows, :]
        gate = logistic(cand)
        high = cand * gate
        skip_ref[rows, :] = d_after * (1.0 - update)
        taken = d_after * update
        d_update = taken * (1.0 - update) * (high - x_ref[rows, :].astype(F32))
        d_tail_ref[rows, wide : wide + width] = d_update.astype(BF16)
        d_tail_ref[rows, wide + width :] = (taken * (gate + high * (1.0 - gate))).astype(BF16)
    gain_grad_ref[...] = gain_grad
    delta = jnp.zeros((count, 1), F32)
    for c in range(0, wide, chunk):
        cols = slice(c, c + chunk)
        d_gated = dot(d_tail_ref[:, wide + width :], out_w_ref[cols, :], ((1,), (1,)))
        attended = attended_ref[:, cols]
        reset = reset_ref[:, cols]
        gate = logistic(reset)
        high = reset * gate
        d_tail_ref[:, cols] = (d_gated * attended * (gate + high * (1.0 - gate))).astype(BF16)
        d_attended = (d_gated * high).astype(BF16)
        d_attended_ref[:, cols] = d_attended
        delta = delta + jnp.sum(d_attended.astype(F32) * attended, axis=1, keepdims=True)
    delta_ref[...] = delta


def middle(gated, attended, reset_pre, update_pre, cand_part, x, cot, w_out, w_up, w_down, gain):
    count, width = x.shape
    wide = gated.shape[1]

    def low(*shape):
        return jax.ShapeDtypeStruct(shape, BF16)

    def full(*shape):
        return jax.ShapeDtypeStruct(shape, F32)

    return pl.pallas_call(
        middle_kernel,
        out_shape=(
            low(count, width), low(count, width), low(count, wide), low(count, wide), low(count, wide + 2 * width),
            full(count, width), full(1, width), low(count, wide), full(count, 1),
        ),
        in_specs=[VMEM()] * 11,
        out_specs=(VMEM(),) * 9,
        scratch_shapes=[pltpu.VMEM((count, width), F32)] * 4,
        compiler_params=pltpu.CompilerParams(vmem_limit_bytes=28 * MIB),
        cost_estimate=BRIEF,
        name="middle",
    )(gated, attended, reset_pre, update_pre, cand_part, x, cot, w_out, w_up, w_down, gain)


def scores_back_kernel(scale, weight_ref, inverse_ref, delta_ref, d_ref, v_ref, q_ref, k_ref, near_ref, far_ref, dq_ref):
    step, steps = pl.program_id(0), pl.num_programs(0)
    d_probs = dot(d_ref[...], v_ref[...], ((1,), (1,)))
    probs = weight_ref[...] * inverse_ref[...]
    d_score = (probs * (d_probs - delta_ref[...]) * scale).astype(BF16)
    d_keys = dot(d_score, q_ref[...], ((0,), (0,))).astype(BF16)

    @pl.when(step < steps // 2)
    def _():
        near_ref[...] = d_keys

    @pl.when(step >= steps // 2)
    def _():
        far_ref[...] = d_keys

    d_queries = dot(d_score, k_ref[...], ((1,), (0,)))

    @pl.when(step == 0)
    def _():
        dq_ref[...] = d_queries

    @pl.when(step > 0)
    def _():
        dq_ref[...] += d_queries


def scores_back(scale, weight, inverse, delta, d_attended, values, queries, keys):
    count, every = weight.shape
    zdim, wide = queries.shape[1], values.shape[1]
    rows = 256
    half = every // rows // 2
    return pl.pallas_call(
        functools.partial(scores_back_kernel, scale),
        grid=(every // rows,),
        out_shape=(
            jax.ShapeDtypeStruct((every // 2, zdim), BF16),
            jax.ShapeDtypeStruct((every // 2, zdim), BF16),
            jax.ShapeDtypeStruct((count, zdim), F32),
        ),
        in_specs=[
            pl.BlockSpec((count, rows), lambda b: (0, b)), whole(count, 1), whole(count, 1), whole(count, wide),
            pl.BlockSpec((rows, wide), lambda b: (b, 0)), whole(count, zdim), pl.BlockSpec((rows, zdim), lambda b: (b, 0)),
        ],
        out_specs=(
            pl.BlockSpec((rows, zdim), lambda b: (jnp.minimum(b, half - 1), 0)),
            pl.BlockSpec((rows, zdim), lambda b: (jnp.maximum(b - half, 0), 0)),
            whole(count, zdim),
        ),
        compiler_params=pltpu.CompilerParams(vmem_limit_bytes=10 * MIB),
        cost_estimate=BRIEF,
        name="scores_back",
    )(in_hbm(weight), inverse, delta, d_attended, in_hbm(values), queries, keys)


def third_kernel(
    next_ref, dq_ref, z_ref, query_ref, key_ref, d_tail_ref, w_ref, mixed_ref, smoothed_ref, normed_ref, decay_ref,
    eta_ref, *refs
):
    *part_refs, dz_ref, zw_ref, d_ref, head_ref, omega_ref, small_ref = refs
    segs, length, width = d_ref.shape
    zdim = dq_ref.shape[1]
    d_keys = sum(part_ref[...].astype(F32) for part_ref in part_refs)
    z, d_queries = z_ref[...], dq_ref[...]
    gate = logistic(z)
    shared = z * gate
    small_ref[0:1, :] = jnp.sum(d_queries * shared, axis=0, keepdims=True)
    small_ref[1:2, :] = jnp.sum(d_queries, axis=0, keepdims=True)
    small_ref[2:3, :] = jnp.sum(d_keys * shared, axis=0, keepdims=True)
    d_shared = d_queries * query_ref[...] + d_keys * key_ref[...]
    dz_ref[...] = (d_shared * (gate + shared * (1.0 - gate))).astype(BF16)
    zw_ref[...] = dot(dz_ref[...], mixed_ref[...], ((0,), (0,))).astype(BF16)
    part = 256
    for c in range(0, width, part):
        cols = slice(c, c + part)
        back = dot(dz_ref[...], w_ref[cols, :zdim], ((1,), (1,))) + dot(d_tail_ref[...], w_ref[cols, zdim:], ((1,), (1,)))
        omega = jnp.zeros((1, part), F32)
        for i in range(segs):
            smoothed = smoothed_ref[i, :, cols]
            gate = logistic(smoothed)
            slope = gate * (1.0 + smoothed * (1.0 - gate))
            d_smoothed = back[i * length : (i + 1) * length] * slope
            d_ref[i, :, cols] = d_smoothed
            omega = omega + jnp.sum(d_smoothed * normed_ref[i, :, cols], axis=0, keepdims=True)
        omega_ref[:, cols] = omega
    part = width // 2
    for c in range(0, width, part):
        cols = slice(c, c + part)
        decay, eta = decay_ref[:, cols], eta_ref[:, cols]

        def eight(block, grads):
            at = pl.multiple_of(length - 8 - block * 8, 8)
            rows = [d_ref[i, pl.ds(at, 8), cols] for i in range(segs)]
            for u in reversed(range(8)):
                grads = tuple(
                    grad * (decay * next_ref[i, at + u]) + eta * rows[i][u : u + 1]
                    for i, grad in enumerate(grads)
                )
            return grads

        zero = jnp.zeros(decay.shape, F32)
        grads = lax.fori_loop(0, length // 8, eight, (zero,) * segs)
        for i in range(segs):
            head_ref[i, :, cols] = grads[i]


def ema_third(
    keep_next, d_queries, z_pre, query_gain, key_gain, d_tail, w_mix, mixed_in, smoothed, normed, decay, eta, *parts
):
    segs, length, width = normed.shape
    count, zdim = z_pre.shape
    return pl.pallas_call(
        third_kernel,
        out_shape=(
            jax.ShapeDtypeStruct((count, zdim), BF16),
            jax.ShapeDtypeStruct((zdim, width), BF16),
            jax.ShapeDtypeStruct(normed.shape, F32),
            jax.ShapeDtypeStruct((segs, *decay.shape), F32),
            jax.ShapeDtypeStruct((1, width), F32),
            jax.ShapeDtypeStruct((3, zdim), F32),
        ),
        in_specs=[SMEM()] + [VMEM()] * (11 + len(parts)),
        out_specs=(VMEM(),) * 6,
        compiler_params=pltpu.CompilerParams(vmem_limit_bytes=20 * MIB),
        cost_estimate=BRIEF,
        name="ema_third",
    )(keep_next, d_queries, z_pre, query_gain, key_gain, d_tail, w_mix, mixed_in, smoothed, normed, decay, eta, *parts)


def half_kernel(halved, half_ref, slot_ref, *refs):
    *refs, low_ref, high_ref = refs
    half = low_ref.shape[0]
    blocks = 2 * half
    at = 0
    for i, kind in enumerate(halved):
        left_ref, right_ref = refs[2 * i], refs[2 * i + 1]
        (count, tall), wide = left_ref.shape, right_ref.shape[1]
        piece = min(count, 2048)
        own_left = slice(None)
        if kind == "left":
            tall //= 2
            own_left = pl.ds(pl.multiple_of(half_ref[0] * tall, 128), tall)
        else:
            wide //= 2
        rows = tall // blocks
        chunk = 384
        for c in range(0, wide, chunk):
            own_right = slice(c, c + chunk)
            if kind == "right":
                own_right = pl.ds(pl.multiple_of(half_ref[0] * wide + c, 128), chunk)
            part = sum(
                dot(left_ref[k : k + piece, own_left], right_ref[k : k + piece, own_right], ((0,), (0,)))
                for k in range(0, count, piece)
            )
            for b in range(blocks):
                slot = slot_ref[b]
                own = part[b * rows : (b + 1) * rows].astype(BF16)

                @pl.when(slot < half)
                def _():
                    low_ref[slot, at : at + rows, c : c + chunk] = own

                @pl.when(slot >= half)
                def _():
                    high_ref[slot - half, at : at + rows, c : c + chunk] = own

        at += rows


def grad_half(half, slots, halved, *pairs):
    blocks = slots.shape[0]
    rows, held = 0, 0
    for i, kind in enumerate(halved):
        left, right = pairs[2 * i], pairs[2 * i + 1]
        rows += left.shape[1] // (2 if kind == "left" else 1) // blocks
        held += 2 * (left.size + right.size) + left.shape[1] * right.shape[1]
        wide = right.shape[1] // (1 if kind == "left" else 2)
    return pl.pallas_call(
        functools.partial(half_kernel, halved),
        out_shape=(jax.ShapeDtypeStruct((blocks // 2, rows, wide), BF16),) * 2,
        in_specs=[SMEM()] * 2 + [VMEM()] * len(pairs),
        out_specs=(VMEM(),) * 2,
        compiler_params=pltpu.CompilerParams(vmem_limit_bytes=held + 8 * MIB),
        cost_estimate=BRIEF,
        name="grad_half",
    )(half, slots, *pairs)


def place_kernel(halved, lead, core_ref, place_ref, own_ref, other_ref, *refs):
    wide = own_ref.shape[2]
    core = core_ref[0]
    own, other = own_ref[0].astype(F32), other_ref[0].astype(F32)
    at = 0
    for kind, out_ref in zip(halved, refs[-len(halved) :], strict=True):
        if kind == "right":
            rows = out_ref.shape[1]
            mine = pl.ds(pl.multiple_of(core * wide, 128), wide)
            others = pl.ds(pl.multiple_of((1 - core) * wide, 128), wide)
            out_ref[0, :, mine] = own[at : at + rows]
            out_ref[0, :, others] = other[at : at + rows]
        else:
            rows = out_ref.shape[2]
            if lead:
                out_ref[:, 0, :, :lead] = jnp.zeros((2, rows, lead), F32)
            out_ref[core, 0, :, lead:] = own[at : at + rows]
            out_ref[1 - core, 0, :, lead:] = other[at : at + rows]
        at += rows


def put_in_place(core, places, halved, talls, lead, own, other, before=()):
    half, rows, wide = own.shape
    blocks = 2 * half
    shapes, specs = [], []
    for kind, tall in zip(halved, talls, strict=True):
        if kind == "right":
            each = tall // blocks
            shapes.append(jax.ShapeDtypeStruct((blocks, each, 2 * wide), F32))
            specs.append(pl.BlockSpec((1, each, 2 * wide), lambda i, core, places: (places[i], 0, 0)))
        else:
            each = tall // 2 // blocks
            shapes.append(jax.ShapeDtypeStruct((2, blocks, each, lead + wide), F32))
            specs.append(pl.BlockSpec((2, 1, each, lead + wide), lambda i, core, places: (0, places[i], 0, 0)))
    block = pl.BlockSpec((1, rows, wide), lambda i, core, places: (i, 0, 0))
    return pl.pallas_call(
        functools.partial(place_kernel, halved, lead),
        out_shape=shapes,
        grid_spec=pltpu.PrefetchScalarGridSpec(
            num_scalar_prefetch=2,
            grid=(half,),
            in_specs=[block, block] + [pl.BlockSpec(memory_space=pl.ANY)] * len(before),
            out_specs=specs,
        ),
        input_output_aliases={4 + i: i for i in range(len(before))},
        compiler_params=pltpu.CompilerParams(vmem_limit_bytes=20 * MIB),
        cost_estimate=BRIEF,
        name="put_in_place",
    )(core, places, own, other, *before)


def after(value, *others):
    return lax.optimization_barrier((value, *others))[0]


def added(one, two):
    return (one.astype(F32) + two.astype(F32)).astype(one.dtype)


CORES = [(0, 1), (1, 0)]


def swapped(part):
    return lax.ppermute(part, "core", CORES)


def across(part, bit):
    chips = lax.axis_size("g") * lax.axis_size("s")
    return lax.ppermute(part, ("g", "s"), [(i, i ^ (1 << bit)) for i in range(chips)])


class Lane:
    def __init__(self, order, back, halved):
        chips = lax.axis_size("g") * lax.axis_size("s")
        bits = chips.bit_length() - 1
        order = list(order) + [bit for bit in range(bits) if bit not in order]
        self.cut, self.rest, self.halved = order[:3], order[3:], halved
        chip = lax.axis_index(("g", "s"))
        self.core = lax.axis_index("core").reshape(1)
        block = jnp.arange(1 << len(self.cut), dtype=jnp.int32)
        count = len(self.cut)
        self.slots = block ^ sum(((chip >> bit) & 1) << (count - 1 - t) for t, bit in enumerate(self.cut))
        self.back = [bit for bit in back if bit in self.cut]
        self.back_slots = sum(
            (((block >> (count - 1 - t)) ^ (chip >> bit)) & 1) << self.back.index(bit) for t, bit in enumerate(self.cut)
        )

    def theirs(self, *pairs):
        self.talls = [left.shape[1] for left in pairs[::2]]
        low, high = grad_half(1 - self.core, self.slots, self.halved, *pairs)
        self.received, self.received_low = swapped(high), swapped(low)
        return high

    def mine(self, *pairs):
        self.low, self.kept = grad_half(self.core, self.slots, self.halved, *pairs)
        self.turn = 0
        return self.kept

    def more(self):
        return self.turn < 2 * len(self.cut) + len(self.rest)

    def near_end(self):
        return self.turn >= 2 * len(self.cut) + len(self.rest) - 1

    def step(self, *others):
        received = after(self.received, *others)
        cut, rest = self.cut, self.rest
        doubled = self.turn - len(cut) - len(rest)
        if self.turn == 0:
            self.sent = added(self.kept, received)
            self.kept = added(self.low, after(self.received_low, self.sent))
            bit = cut[0]
        elif self.turn < len(cut):
            half = self.kept.shape[0] // 2
            self.sent = added(self.kept[half:], received[half:])
            self.kept = added(self.kept[:half], received[:half])
            bit = cut[self.turn]
        elif doubled < 0:
            self.sent = self.kept = added(self.kept, received)
            bit = rest[self.turn - len(cut)]
        elif doubled == 0:
            self.sent = added(self.kept, received)
            bit = self.back[0]
        else:
            self.sent = jnp.concatenate([self.sent, received])
            bit = self.back[doubled]
        self.received = across(self.sent, bit)
        self.turn += 1
        return self.sent

    def end_near(self, last, lead=0):
        self.lead = lead
        other = after(swapped(self.sent), last)
        half = self.sent.shape[0]
        slot = jnp.arange(2 * half, dtype=jnp.int32)
        self.places = jnp.sum(jnp.where(self.back_slots[None] == slot[:, None], slot[None], 0), axis=1, dtype=jnp.int32)
        self.outs = put_in_place(self.core, self.places[:half], self.halved, self.talls, lead, self.sent, other)
        return self.outs[0]

    def arrive(self, *others):
        self.received = after(self.received, *others)
        self.other = swapped(self.received)
        return self.received

    def end(self, last):
        half = self.sent.shape[0]
        outs = put_in_place(
            self.core, self.places[half:], self.halved, self.talls, self.lead,
            self.received, after(self.other, last), self.outs,
        )
        return [out.reshape(tall, -1) for out, tall in zip(outs, self.talls, strict=True)]


def local(
    tokens,
    cotangent,
    doc_lengths,
    attn_gain,
    ema_beta,
    alpha_raw,
    delta_raw,
    ema_eta,
    ema_omega,
    w_value,
    w_mix,
    query_gain,
    query_bias,
    key_gain,
    w_out,
    ffn_gain,
    w_up,
    w_down,
):
    held, seg_len, width = tokens.shape
    planes, around = lax.axis_size("g"), lax.axis_size("s")
    g, s, core = lax.axis_index("g"), lax.axis_index("s"), lax.axis_index("core")
    odd = g % 2
    count = 2 * seg_len
    zdim = query_gain.shape[0]
    vdim = w_value.shape[1]
    scale_factor = zdim ** (-0.5)

    def number(z, x, c):
        return (z * around + x) * 2 + c

    routes = [
        [
            (number(z, x, c), number(2 * c + ((z % 2) ^ a), x, z // 2))
            for z in range(planes)
            for x in range(around)
            for c in range(2)
        ]
        for a in range(2)
    ]

    def to_planes(rows):
        return jnp.concatenate(
            [
                lax.ppermute(lax.dynamic_slice_in_dim(rows, odd ^ a, 1, 0), EVERY, routes[a])
                for a in range(2)
            ]
        )

    def from_planes(segs):
        return [
            lax.ppermute(segs[a : a + 1], EVERY, [(b, a_) for a_, b in routes[a]])
            for a in range(2)
        ]

    def in_order(back):
        return jnp.concatenate(
            [jnp.where(odd == 0, back[0], back[1]), jnp.where(odd == 0, back[1], back[0])]
        )

    def nearby(part, k):
        return lax.ppermute(part, "s", [(i, i ^ k) for i in range(around)])

    def gathered_near(part):
        return jnp.concatenate([part] + [nearby(part, k) for k in range(1, around)])

    def gathered(part):
        near = gathered_near(part)
        return jnp.concatenate([near, swapped(near)])

    hops = range(around.bit_length() - 1)

    def hop_gather(part, hop):
        return jnp.concatenate([part, nearby(part, 1 << hop)])

    def hop_send(parts, hop):
        half = parts.shape[0] // 2
        return parts[:half], nearby(parts[half:], 1 << hop)

    def scattered_near(parts, received):
        mine = added(parts, received).reshape(around, parts.shape[0] // around, *parts.shape[1:])
        return mine, [nearby(mine[k], k) for k in range(1, around)]

    def scattered_sum(mine, received):
        total = mine[0].astype(F32)
        for part in received:
            total = total + part.astype(F32)
        return total

    x_rows = to_planes(tokens)

    other = lax.ppermute(doc_lengths, "core", [(0, 1), (1, 0)])
    lengths = jnp.where(g // 2 == core, doc_lengths[odd], other[odd])
    docs = lengths.shape[0]
    before_it = jnp.arange(docs)[:, None] > jnp.arange(docs)[None, :]
    starts = jnp.sum(jnp.where(before_it, lengths[None, :], 0), axis=1)

    def doc_of(positions):
        return jnp.sum((starts[:, None] <= positions[None, :]).astype(jnp.int32), axis=0) - 1

    def kept_at(positions):
        return 1.0 - jnp.any(starts[:, None] == positions[None, :], axis=0).astype(F32)

    def blocks_of(s_of, core_of):
        return [(2 * core_of + (odd ^ i)) * around + s_of for i in range(2)]

    place = jnp.stack(blocks_of(s, core))
    order = jnp.stack(
        [block for c in range(2) for k in range(around) for block in blocks_of(s ^ k, core ^ c)]
    )
    n_segs = order.shape[0]
    block = jnp.arange(n_segs, dtype=jnp.int32)
    other_core = (block // around // 2) ^ core
    near_slots = (other_core * around + ((block % around) ^ s)) * 2 + ((block // around % 2) ^ odd)
    within = jnp.arange(seg_len, dtype=jnp.int32)
    local_pos = (place[:, None] * seg_len + within).reshape(-1)
    every_pos = (order[:, None] * seg_len + within).reshape(-1)
    keep = kept_at(local_pos).reshape(2, seg_len)
    keep_next = kept_at(local_pos + 1).reshape(2, seg_len)
    row_keep = kept_at(jnp.arange(n_segs * seg_len + 1, dtype=jnp.int32))
    passes = jnp.min(row_keep[:-1].reshape(n_segs, seg_len), axis=1)
    passes_back = jnp.min(row_keep[1:].reshape(n_segs, seg_len), axis=1)

    ema_alpha = jax.nn.sigmoid(alpha_raw)
    ema_delta = jax.nn.sigmoid(delta_raw)
    decay = 1.0 - ema_alpha * ema_delta
    feed_gain = ema_alpha * ema_beta
    long_decay = decay
    reach = 1
    while reach < seg_len:
        long_decay = long_decay * long_decay
        reach *= 2
    gain_row, omega_row = attn_gain[None], ema_omega[None]

    normed_rows, ends = ema_first(keep, x_rows, gain_row, decay, feed_gain)
    near_ends = gathered_near(ends)
    every_end = jnp.concatenate([near_ends, swapped(near_ends)])
    every_x = gathered(after(x_rows, near_ends))
    cot_rows = to_planes(after(cotangent, near_ends))
    smoothed, mixed_in, states_enter = ema_second(
        place, near_slots, passes, keep, normed_rows, every_end, long_decay, decay, feed_gain, ema_eta, omega_row
    )
    mixed_in = mixed_in.reshape(count, width)

    z_pre = dot(mixed_in, w_mix[:, :zdim], ((1,), (0,)))
    shared = jax.nn.silu(z_pre)
    queries = (shared * query_gain + query_bias).astype(BF16)
    keys = (shared * key_gain).astype(BF16)
    every_key = gathered(keys)
    every_normed, values, value_slope = row_values(after(every_x, keys), gain_row, w_value)
    mixed_here = after(mixed_in, keys)
    reset_pre = dot(mixed_here, w_mix[:, zdim : zdim + vdim], ((1,), (0,)))
    update_pre = dot(mixed_here, w_mix[:, zdim + vdim : zdim + vdim + width], ((1,), (0,)))
    cand_part = dot(mixed_here, w_mix[:, zdim + vdim + width :], ((1,), (0,)))

    inputs_x = x_rows.reshape(count, width)
    weight, probs_low, inverse, attended, gated = attend(
        scale_factor, local_pos[:, None], doc_of(local_pos)[:, None], every_pos[None], doc_of(every_pos)[None],
        queries, every_key, values, reset_pre,
    )
    cot_flat = cot_rows.reshape(count, width)
    result, ffn_in, hidden, d_up, d_tail, d_skip, grad_ffn_gain, d_attended, delta_row = middle(
        gated, attended, reset_pre, update_pre, cand_part, inputs_x, cot_flat, w_out, w_up, w_down, ffn_gain[None]
    )
    d_cand = d_tail[:, vdim + width :]

    one, two = Lane((2, 0, 1, 3), (2, 1, 0), ("left", "right")), Lane((1, 0, 2, 3), (0, 1, 2), ("right",))
    three, four = Lane((2, 1, 0, 3), (0, 2, 1), ("left",)), Lane((0, 1, 2, 3), (0, 1, 2), ("left",))

    def all_step(last, *lanes):
        for lane in lanes:
            if lane.more():
                last = lane.step(last)
        return last

    last = one.theirs(gated, d_cand, ffn_in, d_up)
    last = three.theirs(after(mixed_in, last), d_tail)
    keys_sums, keys_far, d_queries = scores_back(
        scale_factor, weight, inverse, after(delta_row, last), d_attended, values, queries, every_key
    )
    keys_swapped = swapped(keys_far)
    last = one.mine(gated, d_cand, after(ffn_in, d_queries), d_up)
    last = one.step(last)
    keys_sums = added(keys_sums, after(keys_swapped, last))
    last = keys_sums
    for hop in reversed(hops):
        keys_kept, keys_near = hop_send(keys_sums, hop)
        if hop == hops[-1]:
            last = three.mine(after(mixed_in, last), d_tail)
            last = three.step(last)
            last = four.theirs(hidden, after(cot_flat, last))
        if hop > 0:
            keys_sums = added(keys_kept, after(keys_near, last))
            last = keys_sums
    last = four.mine(hidden, after(cot_flat, last))
    last = four.step(last)
    d_value_pre, normed_near_part, normed_far = values_back(
        after(probs_low, last), d_attended, value_slope, w_value
    )
    d_z_pre, grad_z, d_smoothed, grad_heads, grad_omega, grad_z_small = ema_third(
        keep_next, d_queries, z_pre, query_gain[None], key_gain[None], d_tail, w_mix, mixed_in, smoothed, normed_rows,
        decay, ema_eta, keys_kept, after(keys_near, d_value_pre),
    )
    heads = grad_heads
    for hop in hops:
        near = nearby(heads, 1 << hop)
        if hop == 0:
            last = two.theirs(every_normed, after(d_value_pre, heads))
            last = four.step(last)
            near = after(near, last)
        if hop == hops[-1]:
            last = two.mine(every_normed, after(d_value_pre, heads))
            near = after(near, last)
        heads = jnp.concatenate([heads, near])
    far = swapped(heads)
    normed_swapped = swapped(after(normed_far, heads))
    last = one.step(heads)
    last = two.step(last)
    every_head = jnp.concatenate([heads, after(far, last)])
    normed_sums = added(normed_near_part, after(normed_swapped, every_head))
    ema_normed, grad_rates = ema_fourth(
        place, near_slots, passes_back, keep, keep_next, d_smoothed, normed_rows, states_enter, every_head,
        long_decay, decay, feed_gain, ema_eta, omega_row, ema_alpha, ema_delta, ema_beta, grad_omega,
    )
    output = from_planes(after(result, grad_rates).reshape(2, seg_len, width))
    last = all_step(grad_rates, three, four, two, one)
    normed_kept, normed_near = hop_send(after(normed_sums, last, *output), hops[-1])
    output = in_order(output)
    last = all_step(last, three, four, two, one)
    for hop in reversed(hops[:-1]):
        last = added(normed_kept, after(normed_near, last))
        normed_kept, normed_near = hop_send(last, hop)
    last = all_step(last, three, four, two, one)
    d_normed = normed_kept.astype(F32) + after(normed_near, last).astype(F32)
    normed_one, inverse_one = norm_parts(inputs_x.astype(F32))
    d_norm_one, grad_attn_gain = norm_back(
        d_normed + ema_normed.reshape(count, width), normed_one, inverse_one, attn_gain
    )
    back = (d_skip + d_norm_one).astype(BF16)
    gains = jnp.concatenate(
        [
            grad_attn_gain[None],
            grad_omega,
            grad_ffn_gain,
            jnp.pad(grad_z_small.reshape(1, -1), ((0, 0), (0, width - 3 * zdim))),
            jnp.zeros((12, width), F32),
        ]
    )
    small = jnp.concatenate([grad_rates, gains.astype(BF16), grad_z])
    tall = small.shape[0] // 2
    small_far = lax.dynamic_slice_in_dim(small, (1 - core) * tall, tall)
    small_own = lax.dynamic_slice_in_dim(small, core * tall, tall)
    small, last = small_own, (small_far,)
    for bit in [None] + list(range((planes * around).bit_length() - 1)):
        small_near = swapped(small_far) if bit is None else across(after(small, *last), bit)
        last = all_step(small, *(lane for lane in (one, three, four, two) if not lane.near_end()))
        small = added(small, after(small_near, last))
        last = (small,)
        if bit == 0:
            sent_back = from_planes(after(back, small).reshape(2, seg_len, width))
        if bit == 1:
            last = (small, *sent_back)
    grad_tokens = in_order(sent_back).astype(F32)
    small_near = swapped(after(small, *last))
    last = small
    while not all(lane.near_end() for lane in (one, two, three, four)):
        last = all_step(last, *(lane for lane in (one, three, four, two) if not lane.near_end()))
    order_of_end = four, one, two, three
    last = all_step(last, *order_of_end)
    ended = {}
    for lane in order_of_end:
        last = lane.end_near(last, zdim if lane is three else 0)
    for lane in order_of_end:
        last = lane.arrive(last)
    for lane in order_of_end:
        ended[lane] = lane.end(last)
        last = ended[lane][0]
    small_near = after(small_near, last)
    small = jnp.where(core == 0, jnp.concatenate([small, small_near]), jnp.concatenate([small_near, small]))
    small = small.astype(F32)
    (grad_wout, grad_up), (grad_value,), (grad_mix,), (grad_down,) = (ended[lane] for lane in (one, two, three, four))
    grad_mix = lax.dynamic_update_slice(grad_mix, small[-zdim:].T, (0, 0))
    n_heads = decay.shape[0]
    grad_beta, grad_alpha, grad_delta, grad_eta = (small[i * n_heads : (i + 1) * n_heads] for i in range(4))
    grad_attn_gain, grad_omega, grad_ffn_gain, last = (small[4 * n_heads + i] for i in range(4))
    grad_qgain, grad_qbias, grad_kgain = (last[i * zdim : (i + 1) * zdim] for i in range(3))
    return (
        output,
        grad_tokens,
        grad_attn_gain,
        grad_beta,
        grad_alpha,
        grad_delta,
        grad_eta,
        grad_omega,
        grad_value,
        grad_mix,
        grad_qgain,
        grad_qbias,
        grad_kgain,
        grad_wout,
        grad_ffn_gain,
        grad_up,
        grad_down,
    )


def solution(mesh):
    devices = mesh.devices
    finer = Mesh(devices.reshape(4, devices.shape[0] // 4, 2), EVERY)
    split = P("core", ("g", "s"), None)
    placed = (split, split, P("core", None)) + (P(),) * 15
    return jax.shard_map(
        local,
        mesh=finer,
        in_specs=placed,
        out_specs=(split, split) + (P(),) * 15,
        check_vma=False,
    )
```
